128 devices in a mesh: row: 8 (over y, core), col: 16 (over x, z).
Axes of the slice: x: 4, y: 4, z: 4, core: 2. Of those that a mesh axis runs over, the one named last changes fastest.
Arguments:
- front: float32 [8, 16, 128, 16, 8, 128], P('row', None, None, 'col'), may hold values from -1 to 3, as said below
- children: bfloat16 [8, 24, 128, 16, 6, 128], P('row', None, None, 'col'), may hold values from -8 to 14, as said below
- child_maps: int32 [2, 96], replicated, may hold values from 0 to 127, as said below
- fill: int32 [128, 128], replicated, may hold values from 0 to 1, as said below
Outputs:
- factored: float32 [8, 16, 128, 16, 8, 128], P('row', None, None, 'col')
The draws below stay inside these ranges and needn't reach their ends.
Inputs may be any that keep to these rules, and one draw needn't show every extreme that they name: `front`: symmetric positive definite. `children`: each child's matrix is symmetric positive definite. `child_maps`: A row's 96 entries are distinct. For each group g, the child tiles g * 16 to (g + 1) * 16 - 1 go, as a cyclic shift, onto one aligned block of 16 parent tiles; in each row one group goes onto the parent tiles 0 to 15. The child tiles that one device holds send at most 1 tile columns to one column of the grid and at most 4 tile rows to one row of the grid, and devices reach both bounds. `fill`: symmetric, with ones on the diagonal.
All inputs are finite; a program needn't handle non-finite values.
Results may differ from the reference program's by a relative error of at most 0.0003.
Values may be sent and summed in bfloat16 or wider, within the bound.
A program may use at most 192 MiB of HBM per device.

```python
import math
import jax
import jax.numpy as jnp
from jax import lax

NP = 16384
NC = 12288
TILE = 128
PANELS = 3
GRID_ROWS = 8
GRID_COLS = 16
HALF_ROWS = 4
TP = 128
TC = 96
PANEL = 512
COL_GROUPS = 6
CHILD_ROWS = 24
PARENT_ROWS = 16
PARENT_COLS = 8


def gram_matrix(factors, diagonal):
    factor_rank = factors.shape[1]
    product = jnp.dot(factors, factors.T, precision=lax.Precision.HIGHEST, preferred_element_type=jnp.float32) / factor_rank
    positions = jnp.arange(factors.shape[0])
    return product + jnp.where(positions[:, None] == positions[None, :], diagonal[None, :], 0.0)


def draw_front(key, part):
    key = jax.random.fold_in(key, 3)
    gaussian_key, diagonal_key = jax.random.split(key)
    gaussian = jax.random.normal(gaussian_key, (NP, NP), jnp.float32)
    diagonal = jax.random.uniform(diagonal_key, (NP,), jnp.float32, 1.0, 2.0)
    spread = 0.375 / math.sqrt(2.0 * NP)
    positions = jnp.arange(NP)
    on_diagonal = positions[:, None] == positions[None, :]
    whole = (gaussian + gaussian.T) * spread + jnp.where(on_diagonal, diagonal[None, :], 0.0)
    return whole.reshape(PARENT_ROWS, GRID_ROWS, TILE, PARENT_COLS, GRID_COLS, TILE).transpose(1, 0, 2, 4, 3, 5)


def draw_children(key, part):
    key = jax.random.fold_in(key, 5)
    factor_rank = 4 * TILE
    halves = []
    for child_index in range(2):
        factor_key = jax.random.fold_in(jax.random.fold_in(key, child_index), 0)
        diagonal_key = jax.random.fold_in(jax.random.fold_in(key, child_index), 2)
        factors = jax.random.normal(factor_key, (NC, factor_rank), jnp.float32)
        diagonal = jax.random.uniform(diagonal_key, (NC,), jnp.float32, 0.5, 1.5)
        whole = gram_matrix(factors, diagonal)
        halves.append(whole.reshape(CHILD_ROWS, HALF_ROWS, TILE, COL_GROUPS, GRID_COLS, TILE).transpose(1, 0, 2, 4, 3, 5))
    return jnp.concatenate(halves, axis=0).astype(jnp.bfloat16)


def draw_child_maps(key, part):
    key = jax.random.fold_in(key, 7)
    per_class = GRID_COLS // HALF_ROWS
    block_count = TP // GRID_COLS
    tables = []
    for child_index in range(2):
        child_key = jax.random.fold_in(key, child_index)
        order_key, shift_key, block_key, place_key = jax.random.split(child_key, 4)
        ranking = jax.random.permutation(order_key, COL_GROUPS)
        lanes = ranking % HALF_ROWS
        members = ranking // HALF_ROWS
        class_keys = jax.random.split(shift_key, HALF_ROWS)
        shuffles = jax.vmap(lambda single_key: jax.random.permutation(single_key, per_class))(class_keys)
        shifts = HALF_ROWS * shuffles[lanes, members % per_class] + lanes
        picked = jax.random.permutation(block_key, block_count)[:COL_GROUPS]
        picked = (picked - picked[0]) % block_count
        blocks = picked[jax.random.permutation(place_key, COL_GROUPS)]
        columns = jnp.arange(GRID_COLS)
        table = (columns[None, :] + shifts[:, None]) % GRID_COLS + GRID_COLS * blocks[:, None]
        tables.append(table.reshape(COL_GROUPS * GRID_COLS))
    return jnp.stack(tables).astype(jnp.int32)


def draw_fill(key, part):
    key = jax.random.fold_in(key, 9)
    marks = jax.random.randint(key, (TP, TP), 0, 4) == 0
    positions = jnp.arange(TP)
    symmetric = marks | marks.T | (positions[:, None] == positions[None, :])
    return symmetric.astype(jnp.int32)


def setup_inputs(seed: int = 0) -> dict:
    key_of = jax.random.split(jax.random.key(seed), 5)
    return {
        "front": draw_front(jax.random.fold_in(key_of[4], 71), 0),
        "children": draw_children(jax.random.fold_in(key_of[4], 71), 0),
        "child_maps": draw_child_maps(jax.random.fold_in(key_of[4], 71), 0),
        "fill": draw_fill(jax.random.fold_in(key_of[4], 71), 0),
    }


def reference(front, children, child_maps, fill):
    natural = front.transpose(1, 0, 2, 4, 3, 5).reshape(TP, TILE, TP, TILE)
    assembled = natural * fill.astype(jnp.float32)[:, None, :, None]
    pieces = children.reshape(2, HALF_ROWS, CHILD_ROWS, TILE, GRID_COLS, COL_GROUPS, TILE)
    pieces = pieces.transpose(0, 2, 1, 3, 5, 4, 6).reshape(2, TC, TILE, TC, TILE)
    for child_index in range(2):
        targets = child_maps[child_index]
        contribution = pieces[child_index].astype(jnp.float32).transpose(0, 2, 1, 3)
        assembled = assembled.at[targets[:, None], :, targets[None, :], :].add(contribution)
    parent = assembled.reshape(NP, NP)
    for panel_index in range(PANELS):
        first_col = panel_index * PANEL
        last_col = first_col + PANEL
        diag_factor = jnp.linalg.cholesky(parent[first_col:last_col, first_col:last_col])
        columns = lax.linalg.triangular_solve(diag_factor, parent[first_col:, first_col:last_col], left_side=False, lower=True, transpose_a=True)
        columns = columns.at[:PANEL].set(diag_factor)
        update = jnp.dot(columns[PANEL:].astype(jnp.float32), columns[PANEL:].T.astype(jnp.float32), precision=lax.Precision.HIGHEST, preferred_element_type=jnp.float32)
        parent = parent.at[last_col:, last_col:].add(-update)
        upper_zero = jnp.zeros((first_col, PANEL), jnp.float32)
        parent = parent.at[:, first_col:last_col].set(jnp.concatenate([upper_zero, columns], axis=0))
    finished = PANELS * PANEL
    parent = parent.at[:finished, finished:].set(0.0)
    return parent.reshape(PARENT_ROWS, GRID_ROWS, TILE, PARENT_COLS, GRID_COLS, TILE).transpose(1, 0, 2, 4, 3, 5)
```

```python
import functools
import jax
import jax.numpy as jnp
from jax import lax
from jax.experimental import pallas as pl
from jax.experimental.pallas import tpu as pltpu
from jax.sharding import PartitionSpec as P

T = 128
NB = 12
RHS = 256
WIDE = NB * T + RHS
HI = lax.Precision.HIGHEST
TDOT = (((0,), (0,)), ((), ()))


def split3(x):
    high = x.astype(jnp.bfloat16).astype(jnp.float32)
    rest = x - high
    mid = rest.astype(jnp.bfloat16).astype(jnp.float32)
    return high, mid, rest - mid


def inverse_factor(work, winv):
    sub = lax.broadcasted_iota(jnp.int32, (8, T), 0)
    lane = lax.broadcasted_iota(jnp.int32, (8, T), 1)
    for b in range(T // 8):
        rows = pl.ds(8 * b, 8)
        pa = work[rows, 0:T]
        pw = work[rows, T : 2 * T]
        cols = [jnp.broadcast_to(pa[:, 8 * b + j : 8 * b + j + 1], (8, T)) for j in range(8)]
        scale = jnp.zeros((8, T), jnp.float32)
        for j in range(8):
            pivot = jnp.broadcast_to(cols[j][j : j + 1, :], (8, T))
            root = lax.rsqrt(pivot)
            root = root * (1.5 - 0.5 * pivot * root * root)
            scale = jnp.where(sub == j, root, scale)
            if j == 7:
                break
            factor = jnp.where(sub > j, cols[j] * (root * root), 0.0)
            pa = pa - factor * jnp.broadcast_to(pa[j : j + 1, :], (8, T))
            pw = pw - factor * jnp.broadcast_to(pw[j : j + 1, :], (8, T))
            for m in range(j + 1, 8):
                cols[m] = cols[m] - factor * jnp.broadcast_to(cols[m][j : j + 1, :], (8, T))
        pw = pw * scale
        winv[rows, :] = pw
        if b < T // 8 - 1:
            pa = jnp.where(lane >= 8 * (b + 1), pa * scale, 0.0)
            left = split3(pa)
            right = split3(jnp.concatenate([pa, pw], axis=1))
            lhs = jnp.concatenate([left[0], left[0], left[1], left[1], left[0], left[2]], axis=0)
            rhs = jnp.concatenate([right[0], right[1], right[0], right[1], right[2], right[0]], axis=0)
            change = lax.dot_general(
                lhs.astype(jnp.bfloat16), rhs.astype(jnp.bfloat16), TDOT, preferred_element_type=jnp.float32
            )
            start = 8 * (b + 1)
            work[start:, :] = work[start:, :] - change[start:, :]


def factor_kernel(lead, rhs, out, mat, work, winv, acc):
    mat[...] = jnp.zeros_like(mat)
    for d in range(NB // 2 + 1):
        for i in range(d, NB):
            tile = lead[i - d, d] if d < 6 else lead[i, 6]
            mat[(i - d) * T : (i - d + 1) * T, i * T : (i + 1) * T] = tile.T if 0 < d < 6 else tile
    for d in range(7, NB):
        for i in range(d, NB):
            mat[(i - d) * T : (i - d + 1) * T, i * T : (i + 1) * T] = lead[i, NB - d]
    mat[:, NB * T :] = rhs[...]
    row_id = lax.broadcasted_iota(jnp.int32, (T, T), 0)
    col_id = lax.broadcasted_iota(jnp.int32, (T, T), 1)
    chunks = WIDE // 256

    @pl.loop(0, NB)
    def _(k):
        k0 = pl.multiple_of(k * T, T)
        kk = pl.ds(k0, T)

        @pl.loop(k // 2, chunks)
        def _(n):
            nn = pl.ds(pl.multiple_of(n * 256, 256), 256)
            acc[...] = mat[kk, nn]

            @pl.loop(0, (k + 3) // 4)
            def _(p):
                pp = pl.ds(pl.multiple_of(p * 512, 512), 512)
                left = mat[pp, kk]
                left = jnp.where(
                    lax.broadcasted_iota(jnp.int32, (512, T), 0) + p * 512 < k0, left, 0.0
                )
                acc[...] -= lax.dot_general(
                    left, mat[pp, nn], TDOT, precision=HI, preferred_element_type=jnp.float32
                )

            mat[kk, nn] = acc[...]

        work[:, 0:T] = mat[kk, kk]
        work[:, T : 2 * T] = jnp.where(row_id == col_id, 1.0, 0.0)
        inverse_factor(work, winv)

        @pl.loop(k // 2, chunks)
        def _(n):
            nn = pl.ds(pl.multiple_of(n * 256, 256), 256)
            mat[kk, nn] = jnp.dot(
                winv[...], mat[kk, nn], precision=HI, preferred_element_type=jnp.float32
            )

    out[...] = mat[:, NB * T :]


def factor(lead, rhs):
    return pl.pallas_call(
        factor_kernel,
        out_shape=jax.ShapeDtypeStruct((NB * T, RHS), jnp.float32),
        in_specs=[pl.BlockSpec(memory_space=pltpu.VMEM)] * 2,
        out_specs=pl.BlockSpec(memory_space=pltpu.VMEM),
        scratch_shapes=[
            pltpu.VMEM((NB * T, WIDE), jnp.float32),
            pltpu.VMEM((T, 2 * T), jnp.float32),
            pltpu.VMEM((T, T), jnp.float32),
            pltpu.VMEM((T, 256), jnp.float32),
        ],
        compiler_params=pltpu.CompilerParams(vmem_limit_bytes=56 * 1024 * 1024),
        cost_estimate=pl.CostEstimate(flops=150_000_000_000, bytes_accessed=10_000_000, transcendentals=0),
    )(lead, rhs)


def gather_tiles(tiles, *index):
    return tiles.at[index].get(mode="promise_in_bounds")


def local(front, children, child_maps, fill):
    n_row = lax.axis_size("row")
    n_col = lax.axis_size("col")
    half = n_row // 2
    r = lax.axis_index("row")
    c = lax.axis_index("col")
    h = r // half
    lane = r % half
    tiles = children[0, :, :, 0].transpose(2, 0, 1, 3)
    groups, child_rows = tiles.shape[:2]
    own = front[0, :, :, 0]
    parent_rows, _, parent_cols, _ = own.shape
    per = n_col // half

    heads = child_maps[:, ::n_col]
    shifts = heads % n_col
    blocks = heads // n_col
    wanted = jnp.arange(n_col)
    by_shift = jnp.argmax(shifts[:, None, :] == wanted[None, :, None], axis=2)
    hits = blocks[:, None, :] == jnp.arange(parent_cols)[None, :, None]
    by_block = jnp.argmax(hits, axis=2)
    has_block = jnp.any(hits, axis=2)
    first = by_block[:, 0]

    fill_rows = lax.dynamic_index_in_dim(fill.reshape(parent_rows, n_row, parent_cols, n_col), r, 1, keepdims=False)
    fill_local = lax.dynamic_index_in_dim(fill_rows, c, 2, keepdims=False).astype(jnp.float32)
    base = own * fill_local[:, None, :, None]

    send_group = by_shift[h][(wanted - c) % n_col]
    lead_rows = lax.dynamic_slice_in_dim(tiles, per * first[h], per, axis=1)
    lead_got = lax.all_to_all(lead_rows[send_group], "col", 0, 0, tiled=True)
    rest_got = lax.all_to_all(tiles[send_group], "col", 0, 0, tiled=True)

    own_blocks = by_block[h]
    source = (c - shifts[h][own_blocks]) % n_col
    lead_blocks = jnp.where(has_block[h][:, None, None, None], lead_got[source], 0)
    strip = lax.all_to_all(lead_blocks, "row", 0, 0, tiled=True).reshape(n_row, per, T, T)
    lead_front = base[:2].transpose(2, 0, 1, 3)
    strip_front = lax.all_to_all(lead_front, "row", 0, 0, tiled=True)
    lead_gather = lax.all_gather(lead_blocks[0], "row", axis=0)
    front_gather = lax.all_gather(lead_front[0], "row", axis=0)

    def lead_column(parts, fronts):
        total = fronts.transpose(1, 0, 2, 3).reshape(n_col, T, T)
        for child in range(2):
            places = (wanted - shifts[child, first[child]]) % n_col
            total += parts[child * half + places % half, places // half].astype(jnp.float32)
        return total

    mine = lead_column(strip, strip_front)[:NB].reshape(NB * T, T)
    corner = lead_column(lead_gather, front_gather)[:NB]
    corner = corner[(c + jnp.arange(NB // 2 + 1)) % NB]
    lead = lax.all_gather(corner, "col", axis=0)
    pairs = [(i * n_col + j, (j % n_row) * n_col + 2 * i + j // n_row) for i in range(n_row) for j in range(n_col)]
    moved = lax.ppermute(mine, ("row", "col"), pairs)
    solved = factor(lead, jnp.concatenate([mine, moved], axis=1))

    exponent = jnp.floor(jnp.log2(jnp.maximum(jnp.max(jnp.abs(solved), axis=0), 1e-30))) + 1.0
    coded = jnp.clip(jnp.round(solved * jnp.exp2(15.0 - exponent)), -32767.0, 32767.0).astype(jnp.int16)
    tagged = jnp.concatenate([coded, jnp.broadcast_to(exponent.astype(jnp.int16), (16, 2 * T))], axis=0)
    right = lax.all_gather(tagged[:, :T], "row", axis=0)
    left = lax.all_gather(tagged[:, T:].T, "col", axis=0)
    left = left.reshape(parent_rows * T, NB * T + 16)
    left_rows = left[:, : NB * T].astype(jnp.float32) * jnp.exp2(left[:, NB * T :][:, :1].astype(jnp.float32) - 15.0)
    right_cols = right[:, : NB * T].astype(jnp.float32) * jnp.exp2(right[:, NB * T :][:, :1].astype(jnp.float32) - 15.0)
    right_cols = right_cols.transpose(1, 0, 2).reshape(NB * T, parent_cols * T)
    update = jnp.dot(left_rows, right_cols, precision=lax.Precision.HIGH, preferred_element_type=jnp.float32)
    update = update.reshape(parent_rows, T, parent_cols, T)

    tile_of = c * n_row + r
    panel = solved[:, T:].reshape(NB, T, T)
    steps = jnp.arange(NB)
    upper = jnp.arange(T)[:, None] <= jnp.arange(T)[None, :]
    keep = (steps < tile_of)[:, None, None] | ((steps == tile_of)[:, None, None] & upper[None])
    panel = jnp.where(keep, panel, 0.0).transpose(0, 2, 1)
    panel = jnp.concatenate([panel, jnp.zeros((n_col - NB, T, T), jnp.float32)], axis=0)
    panel = lax.all_to_all(panel, "col", 0, 0, tiled=True)

    ranks = jnp.sum(
        (shifts[:, None, :] % half == shifts[:, :, None] % half)
        & (jnp.arange(groups)[None, None, :] < jnp.arange(groups)[None, :, None]),
        axis=2,
    )
    rows = jnp.arange(n_row)
    lanes = (lane + shifts[h][None, :]) % half == (rows % half)[:, None]
    slots = jnp.argmax(lanes[:, None, :] & (ranks[h][None, None, :] == jnp.arange(2)[None, :, None]), axis=2)
    turn = (rows[:, None, None] + n_row * jnp.arange(2)[None, None, :] - lane - shifts[h][slots][:, :, None]) % n_col
    send_rows = (per * slots[:, :, None] + turn // half).reshape(n_row, 4)
    send_from = (c - shifts[h]) % n_col
    row_send = rest_got[send_from[None, None, :], send_rows[:, :, None]]
    got = lax.all_to_all(row_send, "row", 0, 0, tiled=True)

    parent = base
    local_rows = jnp.arange(parent_rows)
    for child in range(2):
        group = by_block[child][local_rows // 2]
        place = (r + n_row * (local_rows % 2) - shifts[child][group]) % n_col
        row_slot = 2 * ranks[child][group] + local_rows % 2
        part = got[
            (child * half + place % half)[:, None], row_slot[:, None], by_block[child][None, :]
        ]
        valid = has_block[child][local_rows // 2][:, None] & has_block[child][None, :]
        part = jnp.where(valid[:, :, None, None], part, 0).transpose(0, 2, 1, 3)
        parent = parent + part.astype(jnp.float32)

    result = parent - update
    row_tiles = r + n_row * local_rows
    col_tiles = c + n_col * jnp.arange(parent_cols)
    cleared = (row_tiles < NB)[:, None] & (col_tiles >= NB)[None, :]
    result = jnp.where(cleared[:, None, :, None], 0.0, result)
    result = result.at[:, :, 0].set(jnp.where(c < NB, panel, result[:, :, 0]))
    return result[None, :, :, None]


def solution(mesh):
    placed = (
        P("row", None, None, "col", None, None),
        P("row", None, None, "col", None, None),
        P(),
        P(),
    )
    return jax.shard_map(
        local,
        mesh=mesh,
        in_specs=placed,
        out_specs=P("row", None, None, "col", None, None),
        check_vma=False,
    )
```

```python
import functools
import jax
import jax.numpy as jnp
from jax import lax
from jax.experimental import pallas as pl
from jax.experimental.pallas import tpu as pltpu
from jax.sharding import PartitionSpec as P

T = 128
NB = 12
RHS = 256
WIDE = NB * T + RHS
HI = lax.Precision.HIGHEST
TDOT = (((0,), (0,)), ((), ()))


def split3(x):
    high = x.astype(jnp.bfloat16).astype(jnp.float32)
    rest = x - high
    mid = rest.astype(jnp.bfloat16).astype(jnp.float32)
    return high, mid, rest - mid


def inverse_factor(work, winv):
    sub = lax.broadcasted_iota(jnp.int32, (8, T), 0)
    lane = lax.broadcasted_iota(jnp.int32, (8, T), 1)
    for b in range(T // 8):
        rows = pl.ds(8 * b, 8)
        pa = work[rows, 0:T]
        pw = work[rows, T : 2 * T]
        cols = [jnp.broadcast_to(pa[:, 8 * b + j : 8 * b + j + 1], (8, T)) for j in range(8)]
        scale = jnp.zeros((8, T), jnp.float32)
        for j in range(8):
            pivot = jnp.broadcast_to(cols[j][j : j + 1, :], (8, T))
            root = lax.rsqrt(pivot)
            root = root * (1.5 - 0.5 * pivot * root * root)
            scale = jnp.where(sub == j, root, scale)
            if j == 7:
                break
            factor = jnp.where(sub > j, cols[j] * (root * root), 0.0)
            pa = pa - factor * jnp.broadcast_to(pa[j : j + 1, :], (8, T))
            pw = pw - factor * jnp.broadcast_to(pw[j : j + 1, :], (8, T))
            for m in range(j + 1, 8):
                cols[m] = cols[m] - factor * jnp.broadcast_to(cols[m][j : j + 1, :], (8, T))
        pw = pw * scale
        winv[rows, :] = pw
        if b < T // 8 - 1:
            pa = jnp.where(lane >= 8 * (b + 1), pa * scale, 0.0)
            left = split3(pa)
            right = split3(jnp.concatenate([pa, pw], axis=1))
            lhs = jnp.concatenate([left[0], left[0], left[1], left[1], left[0], left[2]], axis=0)
            rhs = jnp.concatenate([right[0], right[1], right[0], right[1], right[2], right[0]], axis=0)
            change = lax.dot_general(
                lhs.astype(jnp.bfloat16), rhs.astype(jnp.bfloat16), TDOT, preferred_element_type=jnp.float32
            )
            start = 8 * (b + 1)
            work[start:, :] = work[start:, :] - change[start:, :]


MESH = pl.DeviceIdType.MESH
Q = 4
PART = T // Q
GROUPS = 6
ROWS = 24
CODED = NB * T
LEFT = CODED + T
RIGHT = CODED + 16


def exchange_factor_kernel(
    pick, turn, slots, lead, rhs, out, got,
    mat, work, winv, acc, packed, own_sem, col_send, col_recv, row_send, row_recv, *recv,
):
    n_row, n_col = lax.axis_size("row"), lax.axis_size("col")
    r, c = lax.axis_index("row"), lax.axis_index("col")
    barrier = pltpu.get_barrier_semaphore()
    for d in range(1, n_col):
        pl.semaphore_signal(barrier, inc=1, device_id={"col": lax.rem(c + d, n_col)}, device_id_type=MESH)
    for e in range(1, n_row):
        pl.semaphore_signal(barrier, inc=1, device_id={"row": lax.rem(r + e, n_row)}, device_id_type=MESH)
    pl.semaphore_wait(barrier, n_col + n_row - 2)

    def col_copy(q, d):
        return pltpu.make_async_remote_copy(
            src_ref=slots.at[q, d],
            dst_ref=recv[q].at[d],
            send_sem=col_send.at[q, d],
            recv_sem=col_recv.at[q, d],
            device_id={"col": lax.rem(c + d, n_col)},
            device_id_type=MESH,
        )

    def col_own(q):
        return pltpu.make_async_copy(slots.at[q, 0], recv[q].at[0], own_sem.at[q])

    def row_copy(q, e):
        return pltpu.make_async_remote_copy(
            src_ref=packed.at[q, e],
            dst_ref=got.at[q, e],
            send_sem=row_send.at[q, e],
            recv_sem=row_recv.at[q, e],
            device_id={"row": lax.rem(r + e, n_row)},
            device_id_type=MESH,
        )

    def row_own(q):
        return pltpu.make_async_copy(packed.at[q, 0], got.at[q, 0], own_sem.at[Q + q])

    for q in range(Q):
        col_own(q).start()
        for d in range(1, n_col):
            col_copy(q, d).start()

    mat[...] = jnp.zeros_like(mat)
    for d in range(NB // 2 + 1):
        for i in range(d, NB):
            tile = lead[i - d, d] if d < 6 else lead[i, 6]
            mat[(i - d) * T : (i - d + 1) * T, i * T : (i + 1) * T] = tile.T if 0 < d < 6 else tile
    for d in range(7, NB):
        for i in range(d, NB):
            mat[(i - d) * T : (i - d + 1) * T, i * T : (i + 1) * T] = lead[i, NB - d]
    mat[:, NB * T :] = rhs[...]
    row_id = lax.broadcasted_iota(jnp.int32, (T, T), 0)
    col_id = lax.broadcasted_iota(jnp.int32, (T, T), 1)
    chunks = WIDE // 256

    @pl.loop(0, NB)
    def _(k):
        k0 = pl.multiple_of(k * T, T)
        kk = pl.ds(k0, T)

        @pl.loop(k // 2, chunks)
        def _(n):
            nn = pl.ds(pl.multiple_of(n * 256, 256), 256)
            acc[...] = mat[kk, nn]

            @pl.loop(0, (k + 3) // 4)
            def _(p):
                pp = pl.ds(pl.multiple_of(p * 512, 512), 512)
                left = mat[pp, kk]
                left = jnp.where(
                    lax.broadcasted_iota(jnp.int32, (512, T), 0) + p * 512 < k0, left, 0.0
                )
                acc[...] -= lax.dot_general(
                    left, mat[pp, nn], TDOT, precision=HI, preferred_element_type=jnp.float32
                )

            mat[kk, nn] = acc[...]

        work[:, 0:T] = mat[kk, kk]
        work[:, T : 2 * T] = jnp.where(row_id == col_id, 1.0, 0.0)
        inverse_factor(work, winv)

        @pl.loop(k // 2, chunks)
        def _(n):
            nn = pl.ds(pl.multiple_of(n * 256, 256), 256)
            mat[kk, nn] = jnp.dot(
                winv[...], mat[kk, nn], precision=HI, preferred_element_type=jnp.float32
            )

        for q in range(Q):

            @pl.when(k == (q + 1) * (NB // Q) - 1)
            def _(q=q):
                col_own(q).wait()
                for d in range(1, n_col):
                    col_copy(q, d).wait_recv()

                @pl.loop(0, n_row * 4)
                def _(i):
                    for g in range(GROUPS):
                        packed[q, i // 4, i % 4, g] = recv[q][pick[g], turn[i]]

                row_own(q).start()
                for e in range(1, n_row):
                    row_copy(q, e).start()

    out[...] = mat[:, NB * T :]

    for q in range(Q):
        row_own(q).wait()
        for d in range(1, n_col):
            col_copy(q, d).wait_send()
        for e in range(1, n_row):
            row_copy(q, e).wait()


def exchange_factor(pick, turn, slots, lead, rhs):
    n_row, n_col = lax.axis_size("row"), lax.axis_size("col")
    vmem = pl.BlockSpec(memory_space=pltpu.VMEM)
    smem = pl.BlockSpec(memory_space=pltpu.SMEM)
    hbm = pl.BlockSpec(memory_space=pl.ANY)
    dma = pltpu.SemaphoreType.DMA
    return pl.pallas_call(
        exchange_factor_kernel,
        out_shape=(
            jax.ShapeDtypeStruct((NB * T, RHS), jnp.float32),
            jax.ShapeDtypeStruct((Q, n_row, 4, GROUPS, PART, T), jnp.bfloat16),
        ),
        in_specs=[smem, smem, hbm, vmem, vmem],
        out_specs=(vmem, hbm),
        scratch_shapes=[
            pltpu.VMEM((NB * T, WIDE), jnp.float32),
            pltpu.VMEM((T, 2 * T), jnp.float32),
            pltpu.VMEM((T, T), jnp.float32),
            pltpu.VMEM((T, 256), jnp.float32),
            pltpu.VMEM((Q, n_row, 4, GROUPS, PART, T), jnp.bfloat16),
            dma((2 * Q,)),
            dma((Q, n_col)),
            dma((Q, n_col)),
            dma((Q, n_row)),
            dma((Q, n_row)),
        ]
        + [pltpu.VMEM((n_col, ROWS, PART, T), jnp.bfloat16)] * Q,
        compiler_params=pltpu.CompilerParams(
            vmem_limit_bytes=60 * 1024 * 1024, collective_id=0, has_side_effects=True
        ),
    )(pick, turn, slots, lead, rhs)


def update_kernel(
    fill, row_pick, col_pick, left, right, got, front, out,
    lbuf, rbuf, rhi, rlo, lhi, llo, acc, lsend, lrecv, rsend, rrecv,
):
    r, c = lax.axis_index("row"), lax.axis_index("col")
    x, z = c // 4, c % 4
    y, core = r // 2, r % 2
    step = 1 - 2 * core

    def at_col(dx, dz):
        return lax.rem(x + dx + 4, 4) * 4 + lax.rem(z + dz + 4, 4)

    def at_row(dy, flip):
        return lax.rem(y + dy, 4) * 2 + (1 - core if flip else core)

    barrier = pltpu.get_barrier_semaphore()
    for d in (1, -1):
        pl.semaphore_signal(barrier, inc=1, device_id={"col": at_col(d, 0)}, device_id_type=MESH)
        pl.semaphore_signal(barrier, inc=1, device_id={"col": at_col(0, d)}, device_id_type=MESH)
    for dy, flip in ((1, False), (2, False), (3, False), (0, True)):
        pl.semaphore_signal(barrier, inc=1, device_id={"row": at_row(dy, flip)}, device_id_type=MESH)
    pl.semaphore_wait(barrier, 8)

    lbuf[c] = left[...]
    rbuf[r] = right[...]
    sent = []

    def send_left(block, part, target):
        copy = pltpu.make_async_remote_copy(
            src_ref=lbuf.at[block, pl.ds(part * 64, 64)],
            dst_ref=lbuf.at[block, pl.ds(part * 64, 64)],
            send_sem=lsend.at[len(sent)],
            recv_sem=lrecv.at[block, part],
            device_id={"col": target},
            device_id_type=MESH,
        )
        copy.start()
        sent.append(copy)

    def wait_left(block, part):
        pltpu.make_async_remote_copy(
            src_ref=lbuf.at[block, pl.ds(part * 64, 64)],
            dst_ref=lbuf.at[block, pl.ds(part * 64, 64)],
            send_sem=lsend.at[0],
            recv_sem=lrecv.at[block, part],
            device_id={"col": at_col(1, 0)},
            device_id_type=MESH,
        ).wait_recv()

    rsent = []

    def send_right(block, target):
        copy = pltpu.make_async_remote_copy(
            src_ref=rbuf.at[block],
            dst_ref=rbuf.at[block],
            send_sem=rsend.at[len(rsent)],
            recv_sem=rrecv.at[block],
            device_id={"row": target},
            device_id_type=MESH,
        )
        copy.start()
        rsent.append(copy)

    def wait_right(block):
        pltpu.make_async_remote_copy(
            src_ref=rbuf.at[block],
            dst_ref=rbuf.at[block],
            send_sem=rsend.at[0],
            recv_sem=rrecv.at[block],
            device_id={"row": at_row(0, True)},
            device_id_type=MESH,
        ).wait_recv()

    def place(part, along, across):
        return at_col(across, along) if part == 0 else at_col(along, across)

    def assemble(first, last):
        @pl.loop(first * 8, last * 8)
        def _(i):
            li, lj = i // 8, i % 8
            for q in range(Q):
                where = pl.ds((li * T + q * PART) * 8 + lj, PART, stride=8)
                value = front[where, :] * fill[i]
                for child in range(2):
                    entry = got[q, row_pick[child, li], row_pick[2 + child, li], col_pick[child, lj]]
                    valid = row_pick[4 + child, li] * col_pick[2 + child, lj]
                    value = value + jnp.where(valid > 0, entry.astype(jnp.float32), 0.0)
                out[where, :] = value

    for part in range(2):
        send_left(c, part, place(part, 1, 0))
        send_left(c, part, place(part, -1, 0))
    send_right(r, at_row(0, True))
    for dy in (1, 3, 2):
        send_right(r, at_row(dy, False))
    for part in range(2):
        send_left(c, part, place(part, 0, 1))
        send_left(c, part, place(part, 0, -1))
    assemble(0, 4)
    for part in range(2):
        block = place(part, -step, 0)
        wait_left(block, part)
        send_left(block, part, place(part, step, 0))
        send_left(block, part, place(part, 0, 1))
        send_left(block, part, place(part, 0, -1))
    for part in range(2):
        block = place(part, step, 0)
        wait_left(block, part)
        send_left(block, part, place(part, 0, 1))
        send_left(block, part, place(part, 0, -1))
    for dy in (1, 3):
        wait_right(at_row(dy, False))
        send_right(at_row(dy, False), at_row(0, True))
    assemble(4, 8)
    for part in range(2):
        block = place(part, 2, 0)
        wait_left(block, part)
        send_left(block, part, place(part, 0, 1))
        send_left(block, part, place(part, 0, -1))
    for along in (0, -step, step):
        for part in range(2):
            block = place(part, along, -step)
            wait_left(block, part)
            send_left(block, part, place(part, 0, step))
    wait_right(at_row(2, False))
    send_right(at_row(2, False), at_row(0, True))
    assemble(8, 12)
    for part in range(2):
        block = place(part, 2, -step)
        wait_left(block, part)
        send_left(block, part, place(part, 0, step))
    assemble(12, 16)
    for dy in range(4):
        wait_right(at_row(dy, True))
    for along in range(4):
        for across in (step, 2):
            for part in range(2):
                wait_left(place(part, along, across), part)

    def split(coded, scale):
        value = coded.astype(jnp.int32).astype(jnp.float32) * scale
        high = value.astype(jnp.bfloat16)
        return value, high, (value - high.astype(jnp.float32)).astype(jnp.bfloat16)

    @pl.loop(0, 8)
    def _(j):
        scale = jnp.exp2(rbuf[j, CODED:RIGHT, :].astype(jnp.int32).astype(jnp.float32)[0:1, :] - 15.0)
        lanes = pl.ds(pl.multiple_of((j % 2) * T, T), T)

        @pl.loop(0, NB)
        def _(k):
            rows = pl.ds(pl.multiple_of(k * T, T), T)
            _, high, low = split(rbuf[j, rows, :], scale)
            rhi[j // 2, rows, lanes] = high
            rlo[j // 2, rows, lanes] = low

    row_id = lax.broadcasted_iota(jnp.int32, (T, T), 0)
    col_id = lax.broadcasted_iota(jnp.int32, (T, T), 1)
    in_panel = c < NB
    panel_lanes = pl.ds(pl.multiple_of(jnp.minimum(c, NB - 1) * T, T), T)

    @pl.loop(0, 4)
    def _(s):
        @pl.loop(0, 4)
        def _(m):
            li = s * 4 + m
            rows = pl.ds(pl.multiple_of(m * T, T), T)
            scale = jnp.exp2(lbuf[li, :, CODED:LEFT].astype(jnp.int32).astype(jnp.float32) - 15.0)

            @pl.loop(0, NB)
            def _(k):
                lanes = pl.ds(pl.multiple_of(k * T, T), T)
                _, high, low = split(lbuf[li, :, lanes], scale)
                lhi[rows, lanes] = high
                llo[rows, lanes] = low

        @pl.loop(0, 4)
        def _(n):
            total = jnp.dot(lhi[...], rlo[n], preferred_element_type=jnp.float32)
            total += jnp.dot(llo[...], rhi[n], preferred_element_type=jnp.float32)
            total += jnp.dot(lhi[...], rhi[n], preferred_element_type=jnp.float32)
            acc[...] = total

            @pl.loop(0, 8)
            def _(i):
                m, j = i // 2, i % 2
                li, lj = s * 4 + m, n * 2 + j
                row_tile, col_tile = r + 8 * li, c + 16 * lj
                where = pl.ds(li * T * 8 + lj, T, stride=8)
                change = acc[pl.ds(pl.multiple_of(m * T, T), T), pl.ds(pl.multiple_of(j * T, T), T)]
                cleared = (row_tile < NB) & (col_tile >= NB)
                out[where, :] = jnp.where(cleared, 0.0, out[where, :] - change)

    @pl.when(in_panel)
    def _():
        @pl.loop(0, 16)
        def _(li):
            row_tile = r + 8 * li
            scale = jnp.exp2(lbuf[li, :, CODED:LEFT].astype(jnp.int32).astype(jnp.float32) - 15.0)
            value = lbuf[li, :, panel_lanes].astype(jnp.int32).astype(jnp.float32) * scale
            keep = (row_tile > c) | ((row_tile == c) & (row_id >= col_id))
            out[pl.ds(li * T * 8, T, stride=8), :] = jnp.where(keep, value, 0.0)

    for copy in sent + rsent:
        copy.wait_send()


def update(fill, row_pick, col_pick, left, right, got, front):
    vmem = pl.BlockSpec(memory_space=pltpu.VMEM)
    smem = pl.BlockSpec(memory_space=pltpu.SMEM)
    dma = pltpu.SemaphoreType.DMA
    return pl.pallas_call(
        update_kernel,
        out_shape=jax.ShapeDtypeStruct(front.shape, jnp.float32),
        in_specs=[smem] * 3 + [vmem] * 4,
        out_specs=vmem,
        scratch_shapes=[
            pltpu.VMEM((16, T, LEFT), jnp.int16),
            pltpu.VMEM((8, RIGHT, T), jnp.int16),
            pltpu.VMEM((4, CODED, 256), jnp.bfloat16),
            pltpu.VMEM((4, CODED, 256), jnp.bfloat16),
            pltpu.VMEM((4 * T, CODED), jnp.bfloat16),
            pltpu.VMEM((4 * T, CODED), jnp.bfloat16),
            pltpu.VMEM((4 * T, 256), jnp.float32),
            dma((32,)),
            dma((16, 2)),
            dma((8,)),
            dma((8,)),
        ],
        compiler_params=pltpu.CompilerParams(
            vmem_limit_bytes=60 * 1024 * 1024, collective_id=1, has_side_effects=True
        ),
    )(fill, row_pick, col_pick, left, right, got, front)


def gather_tiles(tiles, *index):
    return tiles.at[index].get(mode="promise_in_bounds")


def local(front, children, child_maps, fill):
    n_row = lax.axis_size("row")
    n_col = lax.axis_size("col")
    half = n_row // 2
    r = lax.axis_index("row")
    c = lax.axis_index("col")
    h = r // half
    lane = r % half
    tiles = children[0, :, :, 0].transpose(2, 0, 1, 3)
    groups, child_rows = tiles.shape[:2]
    own = front[0, :, :, 0]
    parent_rows, _, parent_cols, _ = own.shape
    per = n_col // half

    heads = child_maps[:, ::n_col]
    shifts = heads % n_col
    blocks = heads // n_col
    wanted = jnp.arange(n_col)
    by_shift = jnp.argmax(shifts[:, None, :] == wanted[None, :, None], axis=2)
    hits = blocks[:, None, :] == jnp.arange(parent_cols)[None, :, None]
    by_block = jnp.argmax(hits, axis=2)
    has_block = jnp.any(hits, axis=2)
    first = by_block[:, 0]

    fill_rows = lax.dynamic_index_in_dim(fill.reshape(parent_rows, n_row, parent_cols, n_col), r, 1, keepdims=False)
    fill_local = lax.dynamic_index_in_dim(fill_rows, c, 2, keepdims=False).astype(jnp.float32)
    base = own[:2] * fill_local[:2, None, :, None]

    lead_rows = lax.dynamic_slice_in_dim(tiles, per * first[h], per, axis=1)
    send_group = by_shift[h][(wanted - c) % n_col]
    lead_got = lax.all_to_all(lead_rows[send_group], "col", 0, 0, tiled=True)
    parts = tiles.reshape(groups, child_rows, Q, PART, T).transpose(2, 0, 1, 3, 4)
    slots = parts[:, by_shift[h]]

    own_blocks = by_block[h]
    source = (c - shifts[h][own_blocks]) % n_col
    lead_blocks = jnp.where(has_block[h][:, None, None, None], lead_got[source], 0)
    strip = lax.all_to_all(lead_blocks, "row", 0, 0, tiled=True).reshape(n_row, per, T, T)
    lead_front = base.transpose(2, 0, 1, 3)
    strip_front = lax.all_to_all(lead_front, "row", 0, 0, tiled=True)
    lead_gather = lax.all_gather(lead_blocks[0], "row", axis=0)
    front_gather = lax.all_gather(lead_front[0], "row", axis=0)

    def lead_column(parts, fronts):
        total = fronts.transpose(1, 0, 2, 3).reshape(n_col, T, T)
        for child in range(2):
            places = (wanted - shifts[child, first[child]]) % n_col
            total += parts[child * half + places % half, places // half].astype(jnp.float32)
        return total

    mine = lead_column(strip, strip_front)[:NB].reshape(NB * T, T)
    corner = lead_column(lead_gather, front_gather)[:NB]
    corner = corner[(c + jnp.arange(NB // 2 + 1)) % NB]
    lead = lax.all_gather(corner, "col", axis=0)
    pairs = [(i * n_col + j, (j % n_row) * n_col + 2 * i + j // n_row) for i in range(n_row) for j in range(n_col)]
    moved = lax.ppermute(mine, ("row", "col"), pairs)
    ranks = jnp.sum(
        (shifts[:, None, :] % half == shifts[:, :, None] % half)
        & (jnp.arange(groups)[None, None, :] < jnp.arange(groups)[None, :, None]),
        axis=2,
    )
    rows = (r + jnp.arange(n_row)) % n_row
    lanes = (lane + shifts[h][None, :]) % half == (rows % half)[:, None]
    choice = jnp.argmax(lanes[:, None, :] & (ranks[h][None, None, :] == jnp.arange(2)[None, :, None]), axis=2)
    turn = (rows[:, None, None] + n_row * jnp.arange(2)[None, None, :] - lane - shifts[h][choice][:, :, None]) % n_col
    turn = (per * choice[:, :, None] + turn // half).reshape(4 * n_row)
    solved, got = exchange_factor(
        shifts[h].astype(jnp.int32),
        turn.astype(jnp.int32),
        slots,
        lead,
        jnp.concatenate([mine, moved], axis=1),
    )

    exponent = jnp.floor(jnp.log2(jnp.maximum(jnp.max(jnp.abs(solved), axis=0), 1e-30))) + 1.0
    coded = jnp.clip(jnp.round(solved * jnp.exp2(15.0 - exponent)), -32767.0, 32767.0).astype(jnp.int16)
    tag = exponent.astype(jnp.int16)
    right = jnp.concatenate([coded[:, :T], jnp.broadcast_to(tag[:T], (16, T))], axis=0)
    left = jnp.concatenate([coded[:, T:].T, jnp.broadcast_to(tag[T:, None], (T, T))], axis=1)

    local_rows = jnp.arange(parent_rows)
    row_pick, row_slot, row_valid = [], [], []
    for child in range(2):
        group = by_block[child][local_rows // 2]
        place = (r + n_row * (local_rows % 2) - shifts[child][group]) % n_col
        row_pick.append((r - child * half - place % half) % n_row)
        row_slot.append(2 * ranks[child][group] + local_rows % 2)
        row_valid.append(has_block[child][local_rows // 2])
    row_pick = jnp.stack(row_pick + row_slot + row_valid).astype(jnp.int32)
    col_pick = jnp.concatenate([by_block, has_block.astype(by_block.dtype)]).astype(jnp.int32)
    result = update(
        fill_local.reshape(-1), row_pick, col_pick, left, right, got, own.reshape(-1, T)
    )
    return result.reshape(front.shape)


def solution(mesh):
    placed = (
        P("row", None, None, "col", None, None),
        P("row", None, None, "col", None, None),
        P(),
        P(),
    )
    return jax.shard_map(
        local,
        mesh=mesh,
        in_specs=placed,
        out_specs=P("row", None, None, "col", None, None),
        check_vma=False,
    )
```

```python
import functools
import jax
import jax.numpy as jnp
from jax import lax
from jax.experimental import pallas as pl
from jax.experimental.pallas import tpu as pltpu
from jax.sharding import PartitionSpec as P

T = 128
NB = 12
RHS = 256
WIDE = NB * T + RHS
HI = lax.Precision.HIGHEST
TDOT = (((0,), (0,)), ((), ()))


def split3(x):
    high = x.astype(jnp.bfloat16).astype(jnp.float32)
    rest = x - high
    mid = rest.astype(jnp.bfloat16).astype(jnp.float32)
    return high, mid, rest - mid


def inverse_factor(work, winv):
    sub = lax.broadcasted_iota(jnp.int32, (8, T), 0)
    lane = lax.broadcasted_iota(jnp.int32, (8, T), 1)
    for b in range(T // 8):
        rows = pl.ds(8 * b, 8)
        pa = work[rows, 0:T]
        pw = work[rows, T : 2 * T]
        cols = [jnp.broadcast_to(pa[:, 8 * b + j : 8 * b + j + 1], (8, T)) for j in range(8)]
        scale = jnp.zeros((8, T), jnp.float32)
        for j in range(8):
            pivot = jnp.broadcast_to(cols[j][j : j + 1, :], (8, T))
            root = lax.rsqrt(pivot)
            root = root * (1.5 - 0.5 * pivot * root * root)
            scale = jnp.where(sub == j, root, scale)
            if j == 7:
                break
            factor = jnp.where(sub > j, cols[j] * (root * root), 0.0)
            pa = pa - factor * jnp.broadcast_to(pa[j : j + 1, :], (8, T))
            pw = pw - factor * jnp.broadcast_to(pw[j : j + 1, :], (8, T))
            for m in range(j + 1, 8):
                cols[m] = cols[m] - factor * jnp.broadcast_to(cols[m][j : j + 1, :], (8, T))
        pw = pw * scale
        winv[rows, :] = pw
        if b < T // 8 - 1:
            pa = jnp.where(lane >= 8 * (b + 1), pa * scale, 0.0)
            left = split3(pa)
            right = split3(jnp.concatenate([pa, pw], axis=1))
            lhs = jnp.concatenate([left[0], left[0], left[1], left[1], left[0], left[2]], axis=0)
            rhs = jnp.concatenate([right[0], right[1], right[0], right[1], right[2], right[0]], axis=0)
            change = lax.dot_general(
                lhs.astype(jnp.bfloat16), rhs.astype(jnp.bfloat16), TDOT, preferred_element_type=jnp.float32
            )
            start = 8 * (b + 1)
            work[start:, :] = work[start:, :] - change[start:, :]


MESH = pl.DeviceIdType.MESH
Q = 4
PART = T // Q
GROUPS = 6
REST = 20
LEAD_ROWS = 4
CORNER = NB // 2 + 1
CODED = NB * T
LEFT = CODED + T
RIGHT = CODED + 16
X_START = (0, 2, 4, 6)
ROW_START = (3, 6, 8, 11)


def exchange_factor_kernel(
    pick, turn, pair, src_row, src_tile, valid, lead_slots, slots, lead_front, out, got,
    mat, work, winv, acc, packed, lead_recv, strip_send, strip, corner_strip, strip_front, corner_front,
    mine, moved, corner, own_sem, lead_send, lead_got, front_send, front_got, strip_sent, strip_got,
    move_sem, ring_send, ring_got, twin_send, twin_got, z_send, z_got, x_send, x_got, row_send, row_got, *buffers,
):
    n_row, n_col = lax.axis_size("row"), lax.axis_size("col")
    z_recv, x_out, x_recv = buffers[:Q], buffers[Q : 2 * Q], buffers[2 * Q :]
    r, c = lax.axis_index("row"), lax.axis_index("col")
    x, z = c // 4, c % 4
    core = r % 2
    step = 1 - 2 * core
    twin = r + step

    def at_col(dx, dz):
        return lax.rem(x + dx + 4, 4) * 4 + lax.rem(z + dz + 4, 4)

    def row_peer(e):
        return lax.rem(r + e, n_row)

    def remote(src, dst, sent, landed, device):
        return pltpu.make_async_remote_copy(
            src_ref=src, dst_ref=dst, send_sem=sent, recv_sem=landed, device_id=device, device_id_type=MESH
        )

    target_row, target_col = c % n_row, 2 * r + c // n_row
    origin_row, origin_col = c // 2, lax.rem(n_row * c + r, n_col)
    moves = (target_row != r) | (target_col != c)

    barrier = pltpu.get_barrier_semaphore()
    for d in range(1, n_col):
        pl.semaphore_signal(barrier, inc=1, device_id={"col": lax.rem(c + d, n_col)}, device_id_type=MESH)
    for e in range(1, n_row):
        pl.semaphore_signal(barrier, inc=1, device_id={"row": row_peer(e)}, device_id_type=MESH)

    @pl.when(moves)
    def _():
        pl.semaphore_signal(
            barrier, inc=1, device_id={"row": origin_row, "col": origin_col}, device_id_type=MESH
        )

    pl.semaphore_wait(barrier, n_col + n_row - 2 + jnp.where(moves, 1, 0))

    def lead_copy(d):
        return remote(
            lead_slots.at[d], lead_recv.at[d], lead_send.at[d], lead_got.at[d], {"col": lax.rem(c + d, n_col)}
        )

    def front_copy(e, whole):
        if whole:
            return remote(
                lead_front.at[0], corner_front.at[r], front_send.at[1, e], front_got.at[1, r], {"row": row_peer(e)}
            )
        return remote(
            lead_front.at[row_peer(e)], strip_front.at[r], front_send.at[0, e], front_got.at[0, r], {"row": row_peer(e)}
        )

    def strip_copy(e, whole):
        if whole:
            return remote(
                strip_send.at[0], corner_strip.at[r], strip_sent.at[1, e], strip_got.at[1, r], {"row": row_peer(e)}
            )
        return remote(
            strip_send.at[row_peer(e)], strip.at[r], strip_sent.at[0, e], strip_got.at[0, r], {"row": row_peer(e)}
        )

    lead_own = pltpu.make_async_copy(lead_slots.at[0], lead_recv.at[0], own_sem.at[0])
    lead_own.start()
    for d in range(1, n_col):
        lead_copy(d).start()
    for e in range(1, n_row):
        for whole in (False, True):
            front_copy(e, whole).start()
    strip_front[r] = lead_front[r]
    corner_front[r] = lead_front[0]

    def z_copy(q, d):
        return remote(
            slots.at[q, d], z_recv[q].at[d], z_send.at[q, d], z_got.at[q, d], {"col": at_col(0, d)}
        )

    def z_own(q):
        return pltpu.make_async_copy(slots.at[q, 0], z_recv[q].at[0], own_sem.at[1 + q])

    def x_copy(q, d):
        return remote(
            x_out[q].at[d], x_recv[q].at[d], x_send.at[q, d], x_got.at[q, d], {"col": at_col(d, 0)}
        )

    def row_copy(q, e):
        return remote(
            packed.at[q, e], got.at[q, e], row_send.at[q, e], row_got.at[q, e], {"row": row_peer(e)}
        )

    def row_own(q):
        return pltpu.make_async_copy(packed.at[q, 0], got.at[q, 0], own_sem.at[1 + Q + q])

    def z_start(q):
        z_own(q).start()
        for d in range(1, 4):
            z_copy(q, d).start()

    lead_own.wait()
    for d in range(1, n_col):
        lead_copy(d).wait_recv()

    @pl.loop(0, n_row)
    def _(b):
        strip_send[b] = lead_recv[pick[GROUPS + b]]

    for e in range(1, n_row):
        for whole in (False, True):
            strip_copy(e, whole).start()
    strip[r] = strip_send[r]
    corner_strip[r] = strip_send[0]
    z_start(0)
    z_start(1)
    for e in range(1, n_row):
        for whole in (False, True):
            kind, peer = int(whole), row_peer(e)
            remote(
                strip_send.at[0], corner_strip.at[peer], strip_sent.at[kind, e], strip_got.at[kind, peer], {"row": peer}
            ).wait_recv()
            remote(
                lead_front.at[0], corner_front.at[peer], front_send.at[kind, e], front_got.at[kind, peer], {"row": peer}
            ).wait_recv()

    @pl.loop(0, NB)
    def _(j):
        tile = strip_front[j % 8, j // 8]
        for child in range(2):
            part = strip[src_row[child, j], src_tile[child, j]].astype(jnp.float32)
            tile = tile + jnp.where(valid[child] > 0, part, 0.0)
        mine[pl.ds(pl.multiple_of(j * T, T), T), :] = tile

    move = remote(
        mine, moved, move_sem.at[0], move_sem.at[1], {"row": target_row, "col": target_col}
    )
    move_own = pltpu.make_async_copy(mine, moved, move_sem.at[2])

    @pl.when(moves)
    def _():
        move.start()

    @pl.when(jnp.logical_not(moves))
    def _():
        move_own.start()

    @pl.loop(0, CORNER)
    def _(t):
        j = lax.rem(c + t, NB)
        tile = corner_front[j % 8, j // 8]
        for child in range(2):
            tile = tile + corner_strip[src_row[child, j], src_tile[child, j]].astype(jnp.float32)
        corner[c, pl.ds(pl.multiple_of(t * T, T), T), :] = tile

    half_rows = CORNER * T // 2
    part_rows = half_rows // 2
    ring, twins = [], []

    def place(part, along, across):
        return at_col(across, along) if part == 0 else at_col(along, across)

    def piece(block, part, owner):
        return corner.at[block, pl.ds(pl.multiple_of(owner * half_rows + part * part_rows, part_rows), part_rows)]

    def ring_copy(block, part, target):
        ref = piece(block, part, core)
        copy = remote(ref, ref, ring_send.at[len(ring)], ring_got.at[block, part], {"col": target})
        copy.start()
        ring.append(copy)

    def ring_wait(block, part):
        ref = piece(block, part, core)
        remote(ref, ref, ring_send.at[0], ring_got.at[block, part], {"col": at_col(1, 0)}).wait_recv()
        copy = remote(ref, ref, twin_send.at[len(twins)], twin_got.at[block, part], {"row": twin})
        copy.start()
        twins.append(copy)

    for part in range(2):
        ring_copy(c, part, place(part, 1, 0))
        ring_copy(c, part, place(part, -1, 0))
    for part in range(2):
        ring_copy(c, part, place(part, 0, 1))
        ring_copy(c, part, place(part, 0, -1))
    for part in range(2):
        block = place(part, -step, 0)
        ring_wait(block, part)
        ring_copy(block, part, place(part, step, 0))
        ring_copy(block, part, place(part, 0, 1))
        ring_copy(block, part, place(part, 0, -1))
    for part in range(2):
        block = place(part, step, 0)
        ring_wait(block, part)
        ring_copy(block, part, place(part, 0, 1))
        ring_copy(block, part, place(part, 0, -1))
    for part in range(2):
        block = place(part, 2, 0)
        ring_wait(block, part)
        ring_copy(block, part, place(part, 0, 1))
        ring_copy(block, part, place(part, 0, -1))
    for along in (0, -step, step, 2):
        for part in range(2):
            block = place(part, along, -step)
            ring_wait(block, part)
            ring_copy(block, part, place(part, 0, step))
    for along in range(4):
        for across in (step, 2):
            for part in range(2):
                ring_wait(place(part, along, across), part)
    z_start(2)
    z_start(3)
    mat[...] = jnp.zeros_like(mat)
    mat[:, NB * T : NB * T + T] = mine[...]

    @pl.when(moves)
    def _():
        move.wait()

    @pl.when(jnp.logical_not(moves))
    def _():
        move_own.wait()

    mat[:, NB * T + T :] = moved[...]
    for dx in range(4):
        for dz in range(4):
            if dx or dz:
                for part in range(2):
                    block = at_col(dx, dz)
                    ref = piece(block, part, 1 - core)
                    remote(ref, ref, twin_send.at[0], twin_got.at[block, part], {"row": twin}).wait_recv()

    for d in range(NB):
        for i in range(d, NB):
            if d < 6:
                tile = corner[i - d, d * T : (d + 1) * T, :]
                tile = tile.T if d else tile
            else:
                tile = corner[i, (NB - d) * T : (NB - d + 1) * T, :]
            mat[(i - d) * T : (i - d + 1) * T, i * T : (i + 1) * T] = tile
    row_id = lax.broadcasted_iota(jnp.int32, (T, T), 0)
    col_id = lax.broadcasted_iota(jnp.int32, (T, T), 1)
    chunks = WIDE // 256

    @pl.loop(0, NB)
    def _(k):
        k0 = pl.multiple_of(k * T, T)
        kk = pl.ds(k0, T)

        @pl.loop(k // 2, chunks)
        def _(n):
            nn = pl.ds(pl.multiple_of(n * 256, 256), 256)
            acc[...] = mat[kk, nn]

            @pl.loop(0, (k + 3) // 4)
            def _(p):
                pp = pl.ds(pl.multiple_of(p * 512, 512), 512)
                left = mat[pp, kk]
                left = jnp.where(
                    lax.broadcasted_iota(jnp.int32, (512, T), 0) + p * 512 < k0, left, 0.0
                )
                acc[...] -= lax.dot_general(
                    left, mat[pp, nn], TDOT, precision=HI, preferred_element_type=jnp.float32
                )

            mat[kk, nn] = acc[...]

        work[:, 0:T] = mat[kk, kk]
        work[:, T : 2 * T] = jnp.where(row_id == col_id, 1.0, 0.0)
        inverse_factor(work, winv)

        @pl.loop(k // 2, chunks)
        def _(n):
            nn = pl.ds(pl.multiple_of(n * 256, 256), 256)
            mat[kk, nn] = jnp.dot(
                winv[...], mat[kk, nn], precision=HI, preferred_element_type=jnp.float32
            )

        for q in range(Q):

            @pl.when(k == X_START[q])
            def _(q=q):
                z_own(q).wait()
                for d in range(1, 4):
                    z_copy(q, d).wait_recv()

                @pl.loop(0, REST)
                def _(i):
                    for kind in range(4):
                        for d in range(4):
                            into = x_recv[q] if d == 0 else x_out[q]
                            into[d, kind, i] = z_recv[q][kind, pair[d, kind], i]

                for d in range(1, 4):
                    x_copy(q, d).start()

            @pl.when(k == ROW_START[q])
            def _(q=q):
                for d in range(1, 4):
                    x_copy(q, d).wait_recv()

                @pl.loop(0, n_row * 4)
                def _(i):
                    line = turn[i]
                    for g in range(GROUPS):
                        rest = x_recv[q][pick[16 + g], pick[24 + g], jnp.minimum(line, REST - 1)]
                        first = lead_recv[pick[g], jnp.maximum(line - REST, 0), q * PART : (q + 1) * PART]
                        packed[q, i // 4, i % 4, g] = jnp.where(line < REST, rest, first)

                row_own(q).start()
                for e in range(1, n_row):
                    row_copy(q, e).start()

    out[...] = mat[:, NB * T :]

    for d in range(1, n_col):
        lead_copy(d).wait_send()
    for e in range(1, n_row):
        for whole in (False, True):
            front_copy(e, whole).wait_send()
            strip_copy(e, whole).wait_send()
    for copy in ring + twins:
        copy.wait_send()
    for q in range(Q):
        row_own(q).wait()
        for d in range(1, 4):
            z_copy(q, d).wait_send()
            x_copy(q, d).wait_send()
        for e in range(1, n_row):
            row_copy(q, e).wait()


def exchange_factor(tables, lead_slots, slots, lead_front):
    n_row, n_col = lax.axis_size("row"), lax.axis_size("col")
    vmem = pl.BlockSpec(memory_space=pltpu.VMEM)
    smem = pl.BlockSpec(memory_space=pltpu.SMEM)
    hbm = pl.BlockSpec(memory_space=pl.ANY)
    dma = pltpu.SemaphoreType.DMA
    f32, bf16 = jnp.float32, jnp.bfloat16
    return pl.pallas_call(
        exchange_factor_kernel,
        out_shape=(
            jax.ShapeDtypeStruct((NB * T, RHS), f32),
            jax.ShapeDtypeStruct((Q, n_row, 4, GROUPS, PART, T), bf16),
        ),
        in_specs=[smem] * 6 + [hbm, hbm, vmem],
        out_specs=(vmem, hbm),
        scratch_shapes=[
            pltpu.VMEM((NB * T, WIDE), f32),
            pltpu.VMEM((T, 2 * T), f32),
            pltpu.VMEM((T, T), f32),
            pltpu.VMEM((T, 256), f32),
            pltpu.VMEM((Q, n_row, 4, GROUPS, PART, T), bf16),
            pltpu.VMEM((n_col, LEAD_ROWS, T, T), bf16),
            pltpu.VMEM((n_row, LEAD_ROWS, T, T), bf16),
            pltpu.VMEM((n_row, LEAD_ROWS, T, T), bf16),
            pltpu.VMEM((n_row, LEAD_ROWS, T, T), bf16),
            pltpu.VMEM((n_row, 2, T, T), f32),
            pltpu.VMEM((n_row, 2, T, T), f32),
            pltpu.VMEM((NB * T, T), f32),
            pltpu.VMEM((NB * T, T), f32),
            pltpu.VMEM((n_col, CORNER * T, T), f32),
            dma((1 + 2 * Q,)),
            dma((n_col,)),
            dma((n_col,)),
            dma((2, n_row)),
            dma((2, n_row)),
            dma((2, n_row)),
            dma((2, n_row)),
            dma((3,)),
            dma((32,)),
            dma((n_col, 2)),
            dma((32,)),
            dma((n_col, 2)),
            dma((Q, 4)),
            dma((Q, 4)),
            dma((Q, 4)),
            dma((Q, 4)),
            dma((Q, n_row)),
            dma((Q, n_row)),
        ]
        + [pltpu.VMEM((4, 2, REST, PART, T), bf16)] * Q
        + [pltpu.VMEM((4, 4, REST, PART, T), bf16)] * (2 * Q),
        compiler_params=pltpu.CompilerParams(
            vmem_limit_bytes=62 * 1024 * 1024, collective_id=0, has_side_effects=True
        ),
    )(*tables, lead_slots, slots, lead_front)


def update_kernel(
    fill, row_pick, col_pick, left, right, got, front, out,
    lbuf, rbuf, rhi, rlo, lhi, llo, acc, lsend, lrecv, rsend, rrecv,
):
    r, c = lax.axis_index("row"), lax.axis_index("col")
    x, z = c // 4, c % 4
    y, core = r // 2, r % 2
    step = 1 - 2 * core

    def at_col(dx, dz):
        return lax.rem(x + dx + 4, 4) * 4 + lax.rem(z + dz + 4, 4)

    def at_row(dy, flip):
        return lax.rem(y + dy, 4) * 2 + (1 - core if flip else core)

    barrier = pltpu.get_barrier_semaphore()
    for d in (1, -1):
        pl.semaphore_signal(barrier, inc=1, device_id={"col": at_col(d, 0)}, device_id_type=MESH)
        pl.semaphore_signal(barrier, inc=1, device_id={"col": at_col(0, d)}, device_id_type=MESH)
    for dy, flip in ((1, False), (2, False), (3, False), (0, True)):
        pl.semaphore_signal(barrier, inc=1, device_id={"row": at_row(dy, flip)}, device_id_type=MESH)
    pl.semaphore_wait(barrier, 8)

    lbuf[c] = left[...]
    rbuf[r] = right[...]
    sent = []

    def send_left(block, part, target):
        copy = pltpu.make_async_remote_copy(
            src_ref=lbuf.at[block, pl.ds(part * 64, 64)],
            dst_ref=lbuf.at[block, pl.ds(part * 64, 64)],
            send_sem=lsend.at[len(sent)],
            recv_sem=lrecv.at[block, part],
            device_id={"col": target},
            device_id_type=MESH,
        )
        copy.start()
        sent.append(copy)

    def wait_left(block, part):
        pltpu.make_async_remote_copy(
            src_ref=lbuf.at[block, pl.ds(part * 64, 64)],
            dst_ref=lbuf.at[block, pl.ds(part * 64, 64)],
            send_sem=lsend.at[0],
            recv_sem=lrecv.at[block, part],
            device_id={"col": at_col(1, 0)},
            device_id_type=MESH,
        ).wait_recv()

    rsent = []

    def send_right(block, target):
        copy = pltpu.make_async_remote_copy(
            src_ref=rbuf.at[block],
            dst_ref=rbuf.at[block],
            send_sem=rsend.at[len(rsent)],
            recv_sem=rrecv.at[block],
            device_id={"row": target},
            device_id_type=MESH,
        )
        copy.start()
        rsent.append(copy)

    def wait_right(block):
        pltpu.make_async_remote_copy(
            src_ref=rbuf.at[block],
            dst_ref=rbuf.at[block],
            send_sem=rsend.at[0],
            recv_sem=rrecv.at[block],
            device_id={"row": at_row(0, True)},
            device_id_type=MESH,
        ).wait_recv()

    def place(part, along, across):
        return at_col(across, along) if part == 0 else at_col(along, across)

    def assemble(first, last):
        @pl.loop(first * 8, last * 8)
        def _(i):
            li, lj = i // 8, i % 8
            for q in range(Q):
                where = pl.ds((li * T + q * PART) * 8 + lj, PART, stride=8)
                value = front[where, :] * fill[i]
                for child in range(2):
                    entry = got[q, row_pick[child, li], row_pick[2 + child, li], col_pick[child, lj]]
                    valid = row_pick[4 + child, li] * col_pick[2 + child, lj]
                    value = value + jnp.where(valid > 0, entry.astype(jnp.float32), 0.0)
                out[where, :] = value

    for part in range(2):
        send_left(c, part, place(part, 1, 0))
        send_left(c, part, place(part, -1, 0))
    send_right(r, at_row(0, True))
    for dy in (1, 3, 2):
        send_right(r, at_row(dy, False))
    for part in range(2):
        send_left(c, part, place(part, 0, 1))
        send_left(c, part, place(part, 0, -1))
    assemble(0, 4)
    for part in range(2):
        block = place(part, -step, 0)
        wait_left(block, part)
        send_left(block, part, place(part, step, 0))
        send_left(block, part, place(part, 0, 1))
        send_left(block, part, place(part, 0, -1))
    for part in range(2):
        block = place(part, step, 0)
        wait_left(block, part)
        send_left(block, part, place(part, 0, 1))
        send_left(block, part, place(part, 0, -1))
    for dy in (1, 3):
        wait_right(at_row(dy, False))
        send_right(at_row(dy, False), at_row(0, True))
    assemble(4, 8)
    for part in range(2):
        block = place(part, 2, 0)
        wait_left(block, part)
        send_left(block, part, place(part, 0, 1))
        send_left(block, part, place(part, 0, -1))
    for along in (0, -step, step):
        for part in range(2):
            block = place(part, along, -step)
            wait_left(block, part)
            send_left(block, part, place(part, 0, step))
    wait_right(at_row(2, False))
    send_right(at_row(2, False), at_row(0, True))
    assemble(8, 12)
    for part in range(2):
        block = place(part, 2, -step)
        wait_left(block, part)
        send_left(block, part, place(part, 0, step))
    assemble(12, 16)
    for dy in range(4):
        wait_right(at_row(dy, True))
    for along in range(4):
        for across in (step, 2):
            for part in range(2):
                wait_left(place(part, along, across), part)

    def split(coded, scale):
        value = coded.astype(jnp.int32).astype(jnp.float32) * scale
        high = value.astype(jnp.bfloat16)
        return value, high, (value - high.astype(jnp.float32)).astype(jnp.bfloat16)

    @pl.loop(0, 8)
    def _(j):
        scale = jnp.exp2(rbuf[j, CODED:RIGHT, :].astype(jnp.int32).astype(jnp.float32)[0:1, :] - 15.0)
        lanes = pl.ds(pl.multiple_of((j % 2) * T, T), T)

        @pl.loop(0, NB)
        def _(k):
            rows = pl.ds(pl.multiple_of(k * T, T), T)
            _, high, low = split(rbuf[j, rows, :], scale)
            rhi[j // 2, rows, lanes] = high
            rlo[j // 2, rows, lanes] = low

    row_id = lax.broadcasted_iota(jnp.int32, (T, T), 0)
    col_id = lax.broadcasted_iota(jnp.int32, (T, T), 1)
    in_panel = c < NB
    panel_lanes = pl.ds(pl.multiple_of(jnp.minimum(c, NB - 1) * T, T), T)

    @pl.loop(0, 4)
    def _(s):
        @pl.loop(0, 4)
        def _(m):
            li = s * 4 + m
            rows = pl.ds(pl.multiple_of(m * T, T), T)
            scale = jnp.exp2(lbuf[li, :, CODED:LEFT].astype(jnp.int32).astype(jnp.float32) - 15.0)

            @pl.loop(0, NB)
            def _(k):
                lanes = pl.ds(pl.multiple_of(k * T, T), T)
                _, high, low = split(lbuf[li, :, lanes], scale)
                lhi[rows, lanes] = high
                llo[rows, lanes] = low

        @pl.loop(0, 4)
        def _(n):
            total = jnp.dot(lhi[...], rlo[n], preferred_element_type=jnp.float32)
            total += jnp.dot(llo[...], rhi[n], preferred_element_type=jnp.float32)
            total += jnp.dot(lhi[...], rhi[n], preferred_element_type=jnp.float32)
            acc[...] = total

            @pl.loop(0, 8)
            def _(i):
                m, j = i // 2, i % 2
                li, lj = s * 4 + m, n * 2 + j
                row_tile, col_tile = r + 8 * li, c + 16 * lj
                where = pl.ds(li * T * 8 + lj, T, stride=8)
                change = acc[pl.ds(pl.multiple_of(m * T, T), T), pl.ds(pl.multiple_of(j * T, T), T)]
                cleared = (row_tile < NB) & (col_tile >= NB)
                out[where, :] = jnp.where(cleared, 0.0, out[where, :] - change)

    @pl.when(in_panel)
    def _():
        @pl.loop(0, 16)
        def _(li):
            row_tile = r + 8 * li
            scale = jnp.exp2(lbuf[li, :, CODED:LEFT].astype(jnp.int32).astype(jnp.float32) - 15.0)
            value = lbuf[li, :, panel_lanes].astype(jnp.int32).astype(jnp.float32) * scale
            keep = (row_tile > c) | ((row_tile == c) & (row_id >= col_id))
            out[pl.ds(li * T * 8, T, stride=8), :] = jnp.where(keep, value, 0.0)

    for copy in sent + rsent:
        copy.wait_send()


def update(fill, row_pick, col_pick, left, right, got, front):
    vmem = pl.BlockSpec(memory_space=pltpu.VMEM)
    smem = pl.BlockSpec(memory_space=pltpu.SMEM)
    dma = pltpu.SemaphoreType.DMA
    return pl.pallas_call(
        update_kernel,
        out_shape=jax.ShapeDtypeStruct(front.shape, jnp.float32),
        in_specs=[smem] * 3 + [vmem] * 4,
        out_specs=vmem,
        scratch_shapes=[
            pltpu.VMEM((16, T, LEFT), jnp.int16),
            pltpu.VMEM((8, RIGHT, T), jnp.int16),
            pltpu.VMEM((4, CODED, 256), jnp.bfloat16),
            pltpu.VMEM((4, CODED, 256), jnp.bfloat16),
            pltpu.VMEM((4 * T, CODED), jnp.bfloat16),
            pltpu.VMEM((4 * T, CODED), jnp.bfloat16),
            pltpu.VMEM((4 * T, 256), jnp.float32),
            dma((32,)),
            dma((16, 2)),
            dma((8,)),
            dma((8,)),
        ],
        compiler_params=pltpu.CompilerParams(
            vmem_limit_bytes=60 * 1024 * 1024, collective_id=1, has_side_effects=True
        ),
    )(fill, row_pick, col_pick, left, right, got, front)


def local(front, children, child_maps, fill):
    n_row = lax.axis_size("row")
    n_col = lax.axis_size("col")
    half = n_row // 2
    r = lax.axis_index("row")
    c = lax.axis_index("col")
    h = r // half
    lane = r % half
    tiles = children[0, :, :, 0].transpose(2, 0, 1, 3)
    groups, child_rows = tiles.shape[:2]
    own = front[0, :, :, 0]
    parent_rows, _, parent_cols, _ = own.shape
    per = n_col // half

    heads = child_maps[:, ::n_col]
    shifts = heads % n_col
    blocks = heads // n_col
    wanted = jnp.arange(n_col)
    by_shift = jnp.argmax(shifts[:, None, :] == wanted[None, :, None], axis=2)
    hits = blocks[:, None, :] == jnp.arange(parent_cols)[None, :, None]
    by_block = jnp.argmax(hits, axis=2)
    has_block = jnp.any(hits, axis=2)
    first = by_block[:, 0]

    fill_rows = lax.dynamic_index_in_dim(fill.reshape(parent_rows, n_row, parent_cols, n_col), r, 1, keepdims=False)
    fill_local = lax.dynamic_index_in_dim(fill_rows, c, 2, keepdims=False).astype(jnp.float32)
    base = own[:2] * fill_local[:2, None, :, None]

    lead_tiles = lax.dynamic_slice_in_dim(tiles, per * first[h], per, axis=1)
    lead_slots = lead_tiles[by_shift[h]]
    lead_front = base.transpose(2, 0, 1, 3)

    ranks = jnp.sum(
        (shifts[:, None, :] % half == shifts[:, :, None] % half)
        & (jnp.arange(groups)[None, None, :] < jnp.arange(groups)[None, :, None]),
        axis=2,
    )
    my_shifts, my_ranks = shifts[h], ranks[h]
    kinds = my_shifts % 4
    chosen = (kinds[None, None, :] == jnp.arange(4)[:, None, None]) & (
        my_ranks[None, None, :] == jnp.arange(2)[None, :, None]
    )
    by_kind = jnp.argmax(chosen, axis=2)
    lines = (per * (first[h] + 1) + jnp.arange(REST)) % child_rows
    slots = tiles[by_kind[:, :, None], lines[None, None, :]]
    slots = slots.reshape(4, 2, REST, Q, PART, T).transpose(3, 0, 1, 2, 4, 5)
    x, z = c // 4, c % 4
    hops = (my_shifts // 4 + (z < kinds)) % 4
    pair = jnp.sum(
        jnp.where(
            (hops[None, None, :] == jnp.arange(4)[:, None, None])
            & (kinds[None, None, :] == jnp.arange(4)[None, :, None]),
            my_ranks[None, None, :],
            0,
        ),
        axis=2,
    )
    pad = jnp.zeros((2,), jnp.int32)
    pick = jnp.concatenate(
        [my_shifts, my_shifts[by_block[h]], pad, hops, pad, kinds]
    ).astype(jnp.int32)
    places = (wanted[None, :NB] - jnp.take_along_axis(shifts, first[:, None], axis=1)) % n_col
    src_row = half * jnp.arange(2)[:, None] + places % half
    rows = (r + jnp.arange(n_row)) % n_row
    lanes = (lane + my_shifts[None, :]) % half == (rows % half)[:, None]
    choice = jnp.argmax(lanes[:, None, :] & (my_ranks[None, None, :] == jnp.arange(2)[None, :, None]), axis=2)
    turn = (rows[:, None, None] + n_row * jnp.arange(2)[None, None, :] - lane - my_shifts[choice][:, :, None]) % n_col
    turn = (per * choice[:, :, None] + turn // half).reshape(4 * n_row)
    turn = (turn - per * (first[h] + 1)) % child_rows
    tables = [pick, turn, pair, src_row, places // half, has_block[:, r]]
    solved, got = exchange_factor([t.astype(jnp.int32) for t in tables], lead_slots, slots, lead_front)

    exponent = jnp.floor(jnp.log2(jnp.maximum(jnp.max(jnp.abs(solved), axis=0), 1e-30))) + 1.0
    coded = jnp.clip(jnp.round(solved * jnp.exp2(15.0 - exponent)), -32767.0, 32767.0).astype(jnp.int16)
    tag = exponent.astype(jnp.int16)
    right = jnp.concatenate([coded[:, :T], jnp.broadcast_to(tag[:T], (16, T))], axis=0)
    left = jnp.concatenate([coded[:, T:].T, jnp.broadcast_to(tag[T:, None], (T, T))], axis=1)

    local_rows = jnp.arange(parent_rows)
    row_pick, row_slot, row_valid = [], [], []
    for child in range(2):
        group = by_block[child][local_rows // 2]
        place = (r + n_row * (local_rows % 2) - shifts[child][group]) % n_col
        row_pick.append((r - child * half - place % half) % n_row)
        row_slot.append(2 * ranks[child][group] + local_rows % 2)
        row_valid.append(has_block[child][local_rows // 2])
    row_pick = jnp.stack(row_pick + row_slot + row_valid).astype(jnp.int32)
    col_pick = jnp.concatenate([by_block, has_block.astype(by_block.dtype)]).astype(jnp.int32)
    result = update(
        fill_local.reshape(-1), row_pick, col_pick, left, right, got, own.reshape(-1, T)
    )
    return result.reshape(front.shape)


def solution(mesh):
    placed = (
        P("row", None, None, "col", None, None),
        P("row", None, None, "col", None, None),
        P(),
        P(),
    )
    return jax.shard_map(
        local,
        mesh=mesh,
        in_specs=placed,
        out_specs=P("row", None, None, "col", None, None),
        check_vma=False,
    )
```

```python
import functools
import jax
import jax.numpy as jnp
from jax import lax
from jax.experimental import pallas as pl
from jax.experimental.pallas import tpu as pltpu
from jax.sharding import PartitionSpec as P

T = 128
NB = 12
RHS = 256
WIDE = NB * T + RHS
HI = lax.Precision.HIGHEST
TDOT = (((0,), (0,)), ((), ()))


def split3(x):
    high = x.astype(jnp.bfloat16).astype(jnp.float32)
    rest = x - high
    mid = rest.astype(jnp.bfloat16).astype(jnp.float32)
    return high, mid, rest - mid


def inverse_factor(work, winv):
    sub = lax.broadcasted_iota(jnp.int32, (8, T), 0)
    lane = lax.broadcasted_iota(jnp.int32, (8, T), 1)
    for b in range(T // 8):
        rows = pl.ds(8 * b, 8)
        pa = work[rows, 0:T]
        pw = work[rows, T : 2 * T]
        cols = [jnp.broadcast_to(pa[:, 8 * b + j : 8 * b + j + 1], (8, T)) for j in range(8)]
        scale = jnp.zeros((8, T), jnp.float32)
        for j in range(8):
            pivot = jnp.broadcast_to(cols[j][j : j + 1, :], (8, T))
            root = lax.rsqrt(pivot)
            root = root * (1.5 - 0.5 * pivot * root * root)
            scale = jnp.where(sub == j, root, scale)
            if j == 7:
                break
            factor = jnp.where(sub > j, cols[j] * (root * root), 0.0)
            pa = pa - factor * jnp.broadcast_to(pa[j : j + 1, :], (8, T))
            pw = pw - factor * jnp.broadcast_to(pw[j : j + 1, :], (8, T))
            for m in range(j + 1, 8):
                cols[m] = cols[m] - factor * jnp.broadcast_to(cols[m][j : j + 1, :], (8, T))
        pw = pw * scale
        winv[rows, :] = pw
        if b < T // 8 - 1:
            pa = jnp.where(lane >= 8 * (b + 1), pa * scale, 0.0)
            left = split3(pa)
            right = split3(jnp.concatenate([pa, pw], axis=1))
            lhs = jnp.concatenate([left[0], left[0], left[1], left[1], left[0], left[2]], axis=0)
            rhs = jnp.concatenate([right[0], right[1], right[0], right[1], right[2], right[0]], axis=0)
            change = lax.dot_general(
                lhs.astype(jnp.bfloat16), rhs.astype(jnp.bfloat16), TDOT, preferred_element_type=jnp.float32
            )
            start = 8 * (b + 1)
            work[start:, :] = work[start:, :] - change[start:, :]


MESH = pl.DeviceIdType.MESH
Q = 4
PART = T // Q
GROUPS = 6
REST = 20
LEAD_ROWS = 4
CORNER = NB // 2 + 1
CODED = NB * T
LEFT = CODED + T
RIGHT = CODED + 16
X_START = (0, 2, 4, 6)
ROW_START = (3, 6, 8, 11)


def exchange_factor_kernel(
    pick, turn, pair, src_row, src_tile, valid, by_shift, by_kind, first, tiles, lead_front, out, got,
    mat, work, winv, acc, packed, lead_slots, z_out, lead_recv, strip, corner_strip, strip_front, corner_front,
    mine, moved, corner, own_sem, lead_send, lead_got, front_send, front_got, strip_sent, strip_got,
    move_send, move_got, ring_send, ring_got, twin_send, twin_got, z_send, z_got, x_send, x_got, row_send, row_got, *buffers,
):
    n_row, n_col = lax.axis_size("row"), lax.axis_size("col")
    z_recv, x_recv, x_out = buffers[:Q], buffers[Q : 2 * Q], buffers[2 * Q :]
    r, c = lax.axis_index("row"), lax.axis_index("col")
    x, z = c // 4, c % 4
    core = r % 2
    step = 1 - 2 * core
    twin = r + step

    def at_col(dx, dz):
        return lax.rem(x + dx + 4, 4) * 4 + lax.rem(z + dz + 4, 4)

    def row_peer(e):
        return lax.rem(r + e, n_row)

    def remote(src, dst, sent, landed, device):
        return pltpu.make_async_remote_copy(
            src_ref=src, dst_ref=dst, send_sem=sent, recv_sem=landed, device_id=device, device_id_type=MESH
        )

    target_row, target_col = c % n_row, 2 * r + c // n_row
    origin_row, origin_col = c // 2, lax.rem(n_row * c + r, n_col)
    moves = (target_row != r) | (target_col != c)

    barrier = pltpu.get_barrier_semaphore()
    for d in range(1, n_col):
        pl.semaphore_signal(barrier, inc=1, device_id={"col": lax.rem(c + d, n_col)}, device_id_type=MESH)
    for e in range(1, n_row):
        pl.semaphore_signal(barrier, inc=1, device_id={"row": row_peer(e)}, device_id_type=MESH)

    @pl.when(moves)
    def _():
        pl.semaphore_signal(
            barrier, inc=1, device_id={"row": origin_row, "col": origin_col}, device_id_type=MESH
        )

    pl.semaphore_wait(barrier, n_col + n_row - 2 + jnp.where(moves, 1, 0))

    def lead_copy(d):
        return remote(
            lead_slots.at[d], lead_recv.at[d], lead_send.at[d], lead_got.at[d], {"col": lax.rem(c + d, n_col)}
        )

    def front_copy(e, whole):
        if whole:
            return remote(
                lead_front.at[0], corner_front.at[r], front_send.at[1, e], front_got.at[1, r], {"row": row_peer(e)}
            )
        return remote(
            lead_front.at[row_peer(e)], strip_front.at[r], front_send.at[0, e], front_got.at[0, r], {"row": row_peer(e)}
        )

    def strip_copy(e, whole):
        if whole:
            return remote(
                lead_slots.at[0], corner_strip.at[r], strip_sent.at[1, e], strip_got.at[1, r], {"row": row_peer(e)}
            )
        return remote(
            lead_slots.at[row_peer(e)], strip.at[r], strip_sent.at[0, e], strip_got.at[0, r], {"row": row_peer(e)}
        )

    for e in range(1, n_row):
        for whole in (False, True):
            front_copy(e, whole).start()

    @pl.loop(0, n_col)
    def _(d):
        for i in range(LEAD_ROWS):
            lead_slots[d, i] = tiles[LEAD_ROWS * first[0] + i, by_shift[d]]

    for d in range(1, n_col):
        lead_copy(d).start()
    lead_recv[0] = lead_slots[0]
    strip_front[r] = lead_front[r]
    corner_front[r] = lead_front[0]

    def z_copy(q, d):
        return remote(
            z_out.at[q, d - 1], z_recv[q].at[d], z_send.at[q, d], z_got.at[q, d], {"col": at_col(0, d)}
        )

    def x_copy(q, d):
        return remote(
            x_out[q % 2].at[d - 1], x_recv[q].at[d], x_send.at[q, d], x_got.at[q, d], {"col": at_col(d, 0)}
        )

    def row_copy(q, e):
        return remote(
            packed.at[e], got.at[q, e], row_send.at[q, e], row_got.at[q, e], {"row": row_peer(e)}
        )

    def row_own(q):
        return pltpu.make_async_copy(packed.at[0], got.at[q, 0], own_sem.at[q])

    def z_start(q):
        for d in range(1, 4):
            z_copy(q, d).start()

    @pl.loop(0, REST)
    def _(i):
        line = lax.rem(LEAD_ROWS * (first[0] + 1) + i, LEAD_ROWS + REST)
        for a in range(2):
            for q in range(Q):
                part = slice(q * PART, (q + 1) * PART)
                z_recv[q][0, a, i] = tiles[line, by_kind[0, a], part]
                for d in range(1, 4):
                    z_out[q, d - 1, a, i] = tiles[line, by_kind[d, a], part]

    for d in range(1, n_col):
        lead_copy(d).wait()

    @pl.loop(0, n_row)
    def _(b):
        lead_slots[b] = lead_recv[pick[GROUPS + b]]

    for e in range(1, n_row):
        for whole in (False, True):
            strip_copy(e, whole).start()
    strip[r] = lead_slots[r]
    corner_strip[r] = lead_slots[0]
    z_start(0)
    z_start(1)
    for e in range(1, n_row):
        for whole in (False, True):
            kind, peer = int(whole), row_peer(e)
            remote(
                lead_slots.at[0], corner_strip.at[peer], strip_sent.at[kind, e], strip_got.at[kind, peer], {"row": peer}
            ).wait_recv()
            remote(
                lead_front.at[0], corner_front.at[peer], front_send.at[kind, e], front_got.at[kind, peer], {"row": peer}
            ).wait_recv()

    @pl.loop(0, NB)
    def _(j):
        tile = strip_front[j % 8, j // 8]
        for child in range(2):
            part = strip[src_row[child, j], src_tile[child, j]].astype(jnp.float32)
            tile = tile + jnp.where(valid[child] > 0, part, 0.0)
        mine[pl.ds(pl.multiple_of(j * T, T), T), :] = tile

    def move(k):
        rows = pl.ds(pl.multiple_of(k * T, T), T)
        return remote(
            mine.at[rows], moved.at[rows], move_send.at[k], move_got.at[k], {"row": target_row, "col": target_col}
        )

    @pl.loop(0, CORNER)
    def _(t):
        j = lax.rem(c + t, NB)
        tile = corner_front[j % 8, j // 8]
        for child in range(2):
            tile = tile + corner_strip[src_row[child, j], src_tile[child, j]].astype(jnp.float32)
        corner[c, pl.ds(pl.multiple_of(t * T, T), T), :] = tile

    half_rows = CORNER * T // 2
    part_rows = half_rows // 2
    ring, twins = [], []

    def place(part, along, across):
        return at_col(across, along) if part == 0 else at_col(along, across)

    def piece(block, part, owner):
        return corner.at[block, pl.ds(pl.multiple_of(owner * half_rows + part * part_rows, part_rows), part_rows)]

    def ring_copy(block, part, target):
        ref = piece(block, part, core)
        copy = remote(ref, ref, ring_send.at[len(ring)], ring_got.at[block, part], {"col": target})
        copy.start()
        ring.append(copy)

    def ring_wait(block, part):
        ref = piece(block, part, core)
        remote(ref, ref, ring_send.at[0], ring_got.at[block, part], {"col": at_col(1, 0)}).wait_recv()
        copy = remote(ref, ref, twin_send.at[len(twins)], twin_got.at[block, part], {"row": twin})
        copy.start()
        twins.append(copy)

    for part in range(2):
        ring_copy(c, part, place(part, 1, 0))
        ring_copy(c, part, place(part, -1, 0))
    for part in range(2):
        ring_copy(c, part, place(part, 0, 1))
        ring_copy(c, part, place(part, 0, -1))
    for part in range(2):
        block = place(part, -step, 0)
        ring_wait(block, part)
        ring_copy(block, part, place(part, step, 0))
        ring_copy(block, part, place(part, 0, 1))
        ring_copy(block, part, place(part, 0, -1))
    for part in range(2):
        block = place(part, step, 0)
        ring_wait(block, part)
        ring_copy(block, part, place(part, 0, 1))
        ring_copy(block, part, place(part, 0, -1))
    for part in range(2):
        block = place(part, 2, 0)
        ring_wait(block, part)
        ring_copy(block, part, place(part, 0, 1))
        ring_copy(block, part, place(part, 0, -1))
    for along in (0, -step, step, 2):
        for part in range(2):
            block = place(part, along, -step)
            ring_wait(block, part)
            ring_copy(block, part, place(part, 0, step))
    for along in range(4):
        for across in (step, 2):
            for part in range(2):
                ring_wait(place(part, along, across), part)
    @pl.when(moves)
    def _():
        @pl.loop(0, NB)
        def _(k):
            move(k).start()

    z_start(2)
    z_start(3)
    mat[...] = jnp.zeros_like(mat)
    mat[:, NB * T : NB * T + T] = mine[...]

    @pl.when(jnp.logical_not(moves))
    def _():
        mat[:, NB * T + T :] = mine[...]

    for dx in range(4):
        for dz in range(4):
            if dx or dz:
                for part in range(2):
                    block = at_col(dx, dz)
                    ref = piece(block, part, 1 - core)
                    remote(ref, ref, twin_send.at[0], twin_got.at[block, part], {"row": twin}).wait_recv()

    for d in range(NB):
        for i in range(d, NB):
            if d < 6:
                tile = corner[i - d, d * T : (d + 1) * T, :]
                tile = tile.T if d else tile
            else:
                tile = corner[i, (NB - d) * T : (NB - d + 1) * T, :]
            mat[(i - d) * T : (i - d + 1) * T, i * T : (i + 1) * T] = tile
    row_id = lax.broadcasted_iota(jnp.int32, (T, T), 0)
    col_id = lax.broadcasted_iota(jnp.int32, (T, T), 1)
    chunks = WIDE // 256

    @pl.loop(0, NB)
    def _(k):
        k0 = pl.multiple_of(k * T, T)
        kk = pl.ds(k0, T)

        @pl.when(moves)
        def _():
            move(k).wait_recv()
            mat[kk, NB * T + T :] = moved[kk, :]

        @pl.loop(k // 2, chunks)
        def _(n):
            nn = pl.ds(pl.multiple_of(n * 256, 256), 256)
            acc[...] = mat[kk, nn]

            @pl.loop(0, (k + 3) // 4)
            def _(p):
                pp = pl.ds(pl.multiple_of(p * 512, 512), 512)
                left = mat[pp, kk]
                left = jnp.where(
                    lax.broadcasted_iota(jnp.int32, (512, T), 0) + p * 512 < k0, left, 0.0
                )
                acc[...] -= lax.dot_general(
                    left, mat[pp, nn], TDOT, precision=HI, preferred_element_type=jnp.float32
                )

            mat[kk, nn] = acc[...]

        work[:, 0:T] = mat[kk, kk]
        work[:, T : 2 * T] = jnp.where(row_id == col_id, 1.0, 0.0)
        inverse_factor(work, winv)

        @pl.loop(k // 2, chunks)
        def _(n):
            nn = pl.ds(pl.multiple_of(n * 256, 256), 256)
            mat[kk, nn] = jnp.dot(
                winv[...], mat[kk, nn], precision=HI, preferred_element_type=jnp.float32
            )

        for q in range(Q):

            @pl.when(k == X_START[q])
            def _(q=q):
                for d in range(1, 4):
                    z_copy(q, d).wait_recv()
                    if q >= 2:
                        x_copy(q - 2, d).wait_send()

                @pl.loop(0, REST)
                def _(i):
                    for kind in range(4):
                        for d in range(4):
                            tile = z_recv[q][kind, pair[d, kind], i]
                            if d == 0:
                                x_recv[q][d, kind, i] = tile
                            else:
                                x_out[q % 2][d - 1, kind, i] = tile

                for d in range(1, 4):
                    x_copy(q, d).start()

            @pl.when(k == ROW_START[q])
            def _(q=q):
                for d in range(1, 4):
                    x_copy(q, d).wait_recv()
                if q >= 1:
                    row_own(q - 1).wait()
                    for e in range(1, n_row):
                        row_copy(q - 1, e).wait_send()

                @pl.loop(0, n_row * 4)
                def _(i):
                    line = turn[i]
                    for g in range(GROUPS):
                        rest = x_recv[q][pick[16 + g], pick[24 + g], jnp.minimum(line, REST - 1)]
                        first = lead_recv[pick[g], jnp.maximum(line - REST, 0), q * PART : (q + 1) * PART]
                        packed[i // 4, i % 4, g] = jnp.where(line < REST, rest, first)

                row_own(q).start()
                for e in range(1, n_row):
                    row_copy(q, e).start()

    out[...] = mat[:, NB * T :]

    for e in range(1, n_row):
        for whole in (False, True):
            front_copy(e, whole).wait_send()
            strip_copy(e, whole).wait_send()
    for copy in ring + twins:
        copy.wait_send()
    for q in range(Q):
        for d in range(1, 4):
            z_copy(q, d).wait_send()
        if q >= 2:
            for d in range(1, 4):
                x_copy(q, d).wait_send()
        if q == Q - 1:
            row_own(q).wait()
            for e in range(1, n_row):
                row_copy(q, e).wait_send()
        for e in range(1, n_row):
            row_copy(q, e).wait_recv()

    @pl.when(moves)
    def _():
        @pl.loop(0, NB)
        def _(k):
            move(k).wait_send()


def exchange_factor(tables, tiles, lead_front):
    n_row, n_col = lax.axis_size("row"), lax.axis_size("col")
    vmem = pl.BlockSpec(memory_space=pltpu.VMEM)
    smem = pl.BlockSpec(memory_space=pltpu.SMEM)
    hbm = pl.BlockSpec(memory_space=pl.ANY)
    dma = pltpu.SemaphoreType.DMA
    f32, bf16 = jnp.float32, jnp.bfloat16
    return pl.pallas_call(
        exchange_factor_kernel,
        out_shape=(
            jax.ShapeDtypeStruct((NB * T, RHS), f32),
            jax.ShapeDtypeStruct((Q, n_row, 4, GROUPS, PART, T), bf16),
        ),
        in_specs=[smem] * 9 + [vmem, vmem],
        out_specs=(vmem, hbm),
        scratch_shapes=[
            pltpu.VMEM((NB * T, WIDE), f32),
            pltpu.VMEM((T, 2 * T), f32),
            pltpu.VMEM((T, T), f32),
            pltpu.VMEM((T, 256), f32),
            pltpu.VMEM((n_row, 4, GROUPS, PART, T), bf16),
            pltpu.VMEM((n_col, LEAD_ROWS, T, T), bf16),
            pltpu.VMEM((Q, 3, 2, REST, PART, T), bf16),
            pltpu.VMEM((n_col, LEAD_ROWS, T, T), bf16),
            pltpu.VMEM((n_row, LEAD_ROWS, T, T), bf16),
            pltpu.VMEM((n_row, LEAD_ROWS, T, T), bf16),
            pltpu.VMEM((n_row, 2, T, T), f32),
            pltpu.VMEM((n_row, 2, T, T), f32),
            pltpu.VMEM((NB * T, T), f32),
            pltpu.VMEM((NB * T, T), f32),
            pltpu.VMEM((n_col, CORNER * T, T), f32),
            dma((Q,)),
            dma((n_col,)),
            dma((n_col,)),
            dma((2, n_row)),
            dma((2, n_row)),
            dma((2, n_row)),
            dma((2, n_row)),
            dma((NB,)),
            dma((NB,)),
            dma((32,)),
            dma((n_col, 2)),
            dma((32,)),
            dma((n_col, 2)),
            dma((Q, 4)),
            dma((Q, 4)),
            dma((Q, 4)),
            dma((Q, 4)),
            dma((Q, n_row)),
            dma((Q, n_row)),
        ]
        + [pltpu.VMEM((4, 2, REST, PART, T), bf16)] * Q
        + [pltpu.VMEM((4, 4, REST, PART, T), bf16)] * Q
        + [pltpu.VMEM((3, 4, REST, PART, T), bf16)] * 2,
        compiler_params=pltpu.CompilerParams(
            vmem_limit_bytes=62 * 1024 * 1024, collective_id=0, has_side_effects=True
        ),
    )(*tables, tiles, lead_front)


def update_kernel(
    fill, row_pick, col_pick, left, right, got, front, out,
    lbuf, rbuf, rhi, rlo, lhi, llo, acc, lsend, lrecv, rsend, rrecv,
):
    r, c = lax.axis_index("row"), lax.axis_index("col")
    x, z = c // 4, c % 4
    y, core = r // 2, r % 2
    step = 1 - 2 * core

    def at_col(dx, dz):
        return lax.rem(x + dx + 4, 4) * 4 + lax.rem(z + dz + 4, 4)

    def at_row(dy, flip):
        return lax.rem(y + dy, 4) * 2 + (1 - core if flip else core)

    barrier = pltpu.get_barrier_semaphore()
    for d in (1, -1):
        pl.semaphore_signal(barrier, inc=1, device_id={"col": at_col(d, 0)}, device_id_type=MESH)
        pl.semaphore_signal(barrier, inc=1, device_id={"col": at_col(0, d)}, device_id_type=MESH)
    for dy, flip in ((1, False), (2, False), (3, False), (0, True)):
        pl.semaphore_signal(barrier, inc=1, device_id={"row": at_row(dy, flip)}, device_id_type=MESH)
    pl.semaphore_wait(barrier, 8)

    lbuf[c] = left[...]
    rbuf[r] = right[...]
    sent = []

    def send_left(block, part, target):
        copy = pltpu.make_async_remote_copy(
            src_ref=lbuf.at[block, pl.ds(part * 64, 64)],
            dst_ref=lbuf.at[block, pl.ds(part * 64, 64)],
            send_sem=lsend.at[len(sent)],
            recv_sem=lrecv.at[block, part],
            device_id={"col": target},
            device_id_type=MESH,
        )
        copy.start()
        sent.append(copy)

    def wait_left(block, part):
        pltpu.make_async_remote_copy(
            src_ref=lbuf.at[block, pl.ds(part * 64, 64)],
            dst_ref=lbuf.at[block, pl.ds(part * 64, 64)],
            send_sem=lsend.at[0],
            recv_sem=lrecv.at[block, part],
            device_id={"col": at_col(1, 0)},
            device_id_type=MESH,
        ).wait_recv()

    rsent = []

    def send_right(block, target):
        copy = pltpu.make_async_remote_copy(
            src_ref=rbuf.at[block],
            dst_ref=rbuf.at[block],
            send_sem=rsend.at[len(rsent)],
            recv_sem=rrecv.at[block],
            device_id={"row": target},
            device_id_type=MESH,
        )
        copy.start()
        rsent.append(copy)

    def wait_right(block):
        pltpu.make_async_remote_copy(
            src_ref=rbuf.at[block],
            dst_ref=rbuf.at[block],
            send_sem=rsend.at[0],
            recv_sem=rrecv.at[block],
            device_id={"row": at_row(0, True)},
            device_id_type=MESH,
        ).wait_recv()

    def place(part, along, across):
        return at_col(across, along) if part == 0 else at_col(along, across)

    def assemble(first, last):
        @pl.loop(first * 8, last * 8)
        def _(i):
            li, lj = i // 8, i % 8
            for q in range(Q):
                where = pl.ds((li * T + q * PART) * 8 + lj, PART, stride=8)
                value = front[where, :] * fill[i]
                for child in range(2):
                    entry = got[q, row_pick[child, li], row_pick[2 + child, li], col_pick[child, lj]]
                    valid = row_pick[4 + child, li] * col_pick[2 + child, lj]
                    value = value + jnp.where(valid > 0, entry.astype(jnp.float32), 0.0)
                out[where, :] = value

    for part in range(2):
        send_left(c, part, place(part, 1, 0))
        send_left(c, part, place(part, -1, 0))
    send_right(r, at_row(0, True))
    for dy in (1, 3, 2):
        send_right(r, at_row(dy, False))
    for part in range(2):
        send_left(c, part, place(part, 0, 1))
        send_left(c, part, place(part, 0, -1))
    assemble(0, 4)
    for part in range(2):
        block = place(part, -step, 0)
        wait_left(block, part)
        send_left(block, part, place(part, step, 0))
        send_left(block, part, place(part, 0, 1))
        send_left(block, part, place(part, 0, -1))
    for part in range(2):
        block = place(part, step, 0)
        wait_left(block, part)
        send_left(block, part, place(part, 0, 1))
        send_left(block, part, place(part, 0, -1))
    for dy in (1, 3):
        wait_right(at_row(dy, False))
        send_right(at_row(dy, False), at_row(0, True))
    assemble(4, 8)
    for part in range(2):
        block = place(part, 2, 0)
        wait_left(block, part)
        send_left(block, part, place(part, 0, 1))
        send_left(block, part, place(part, 0, -1))
    wait_right(at_row(2, False))
    send_right(at_row(2, False), at_row(0, True))
    assemble(8, 16)
    for dy in range(4):
        wait_right(at_row(dy, True))

    def split(coded, scale):
        value = coded.astype(jnp.int32).astype(jnp.float32) * scale
        high = value.astype(jnp.bfloat16)
        return high, (value - high.astype(jnp.float32)).astype(jnp.bfloat16)

    @pl.loop(0, 8)
    def _(j):
        scale = jnp.exp2(rbuf[j, CODED:RIGHT, :].astype(jnp.int32).astype(jnp.float32)[0:1, :] - 15.0)
        lanes = pl.ds(pl.multiple_of((j % 2) * T, T), T)

        @pl.loop(0, NB)
        def _(k):
            rows = pl.ds(pl.multiple_of(k * T, T), T)
            rhi[j // 2, rows, lanes], rlo[j // 2, rows, lanes] = split(rbuf[j, rows, :], scale)

    def subtract(pieces):
        for m, (li, part) in enumerate(pieces):
            source = pl.ds(part * 64, 64)
            scale = jnp.exp2(lbuf[li, source, CODED:LEFT].astype(jnp.int32).astype(jnp.float32) - 15.0)

            @pl.loop(0, NB)
            def _(k, m=m, li=li, source=source, scale=scale):
                lanes = pl.ds(pl.multiple_of(k * T, T), T)
                high, low = split(lbuf[li, source, lanes], scale)
                lhi[m * 64 : (m + 1) * 64, lanes] = high
                llo[m * 64 : (m + 1) * 64, lanes] = low

        @pl.loop(0, 4)
        def _(n):
            total = jnp.dot(lhi[...], rlo[n], preferred_element_type=jnp.float32)
            total += jnp.dot(llo[...], rhi[n], preferred_element_type=jnp.float32)
            total += jnp.dot(lhi[...], rhi[n], preferred_element_type=jnp.float32)
            acc[...] = total
            for m, (li, part) in enumerate(pieces):
                for j in range(2):
                    lj = n * 2 + j
                    where = pl.ds((li * T + part * 64) * 8 + lj, 64, stride=8)
                    change = acc[m * 64 : (m + 1) * 64, j * T : (j + 1) * T]
                    cleared = (r + 8 * li < NB) & (c + 16 * lj >= NB)
                    out[where, :] = jnp.where(cleared, 0.0, out[where, :] - change)

    def arrived(across):
        return [(place(part, along, across), part) for part in range(2) for along in (0, -step, step, 2)]

    subtract(arrived(0))
    for block, part in arrived(-step):
        wait_left(block, part)
        send_left(block, part, place(part, 0, step))
    subtract(arrived(-step))
    for across in (step, 2):
        for block, part in arrived(across):
            wait_left(block, part)
        subtract(arrived(across))

    row_id = lax.broadcasted_iota(jnp.int32, (T, T), 0)
    col_id = lax.broadcasted_iota(jnp.int32, (T, T), 1)
    panel_lanes = pl.ds(pl.multiple_of(jnp.minimum(c, NB - 1) * T, T), T)

    @pl.when(c < NB)
    def _():
        @pl.loop(0, 16)
        def _(li):
            row_tile = r + 8 * li
            scale = jnp.exp2(lbuf[li, :, CODED:LEFT].astype(jnp.int32).astype(jnp.float32) - 15.0)
            value = lbuf[li, :, panel_lanes].astype(jnp.int32).astype(jnp.float32) * scale
            keep = (row_tile > c) | ((row_tile == c) & (row_id >= col_id))
            out[pl.ds(li * T * 8, T, stride=8), :] = jnp.where(keep, value, 0.0)

    for copy in sent + rsent:
        copy.wait_send()


def update(fill, row_pick, col_pick, left, right, got, front):
    vmem = pl.BlockSpec(memory_space=pltpu.VMEM)
    smem = pl.BlockSpec(memory_space=pltpu.SMEM)
    dma = pltpu.SemaphoreType.DMA
    return pl.pallas_call(
        update_kernel,
        out_shape=jax.ShapeDtypeStruct(front.shape, jnp.float32),
        in_specs=[smem] * 3 + [vmem] * 4,
        out_specs=vmem,
        scratch_shapes=[
            pltpu.VMEM((16, T, LEFT), jnp.int16),
            pltpu.VMEM((8, RIGHT, T), jnp.int16),
            pltpu.VMEM((4, CODED, 256), jnp.bfloat16),
            pltpu.VMEM((4, CODED, 256), jnp.bfloat16),
            pltpu.VMEM((4 * T, CODED), jnp.bfloat16),
            pltpu.VMEM((4 * T, CODED), jnp.bfloat16),
            pltpu.VMEM((4 * T, 256), jnp.float32),
            dma((32,)),
            dma((16, 2)),
            dma((8,)),
            dma((8,)),
        ],
        compiler_params=pltpu.CompilerParams(
            vmem_limit_bytes=60 * 1024 * 1024, collective_id=1, has_side_effects=True
        ),
    )(fill, row_pick, col_pick, left, right, got, front)


def local(front, children, child_maps, fill):
    n_row = lax.axis_size("row")
    n_col = lax.axis_size("col")
    half = n_row // 2
    r = lax.axis_index("row")
    c = lax.axis_index("col")
    h = r // half
    lane = r % half
    tiles = children[0, :, :, 0].transpose(0, 2, 1, 3)
    child_rows, groups = tiles.shape[:2]
    own = front[0, :, :, 0]
    parent_rows, _, parent_cols, _ = own.shape
    per = n_col // half

    heads = child_maps[:, ::n_col]
    shifts = heads % n_col
    blocks = heads // n_col
    wanted = jnp.arange(n_col)
    by_shift = jnp.argmax(shifts[:, None, :] == wanted[None, :, None], axis=2)
    hits = blocks[:, None, :] == jnp.arange(parent_cols)[None, :, None]
    by_block = jnp.argmax(hits, axis=2)
    has_block = jnp.any(hits, axis=2)
    first = by_block[:, 0]

    fill_rows = lax.dynamic_index_in_dim(fill.reshape(parent_rows, n_row, parent_cols, n_col), r, 1, keepdims=False)
    fill_local = lax.dynamic_index_in_dim(fill_rows, c, 2, keepdims=False).astype(jnp.float32)
    base = own[:2] * fill_local[:2, None, :, None]

    lead_front = base.transpose(2, 0, 1, 3)

    ranks = jnp.sum(
        (shifts[:, None, :] % half == shifts[:, :, None] % half)
        & (jnp.arange(groups)[None, None, :] < jnp.arange(groups)[None, :, None]),
        axis=2,
    )
    my_shifts, my_ranks = shifts[h], ranks[h]
    kinds = my_shifts % 4
    chosen = (kinds[None, None, :] == jnp.arange(4)[:, None, None]) & (
        my_ranks[None, None, :] == jnp.arange(2)[None, :, None]
    )
    by_kind = jnp.argmax(chosen, axis=2)
    x, z = c // 4, c % 4
    hops = (my_shifts // 4 + (z < kinds)) % 4
    pair = jnp.sum(
        jnp.where(
            (hops[None, None, :] == jnp.arange(4)[:, None, None])
            & (kinds[None, None, :] == jnp.arange(4)[None, :, None]),
            my_ranks[None, None, :],
            0,
        ),
        axis=2,
    )
    pad = jnp.zeros((2,), jnp.int32)
    pick = jnp.concatenate(
        [my_shifts, my_shifts[by_block[h]], pad, hops, pad, kinds]
    ).astype(jnp.int32)
    places = (wanted[None, :NB] - jnp.take_along_axis(shifts, first[:, None], axis=1)) % n_col
    src_row = half * jnp.arange(2)[:, None] + places % half
    rows = (r + jnp.arange(n_row)) % n_row
    lanes = (lane + my_shifts[None, :]) % half == (rows % half)[:, None]
    choice = jnp.argmax(lanes[:, None, :] & (my_ranks[None, None, :] == jnp.arange(2)[None, :, None]), axis=2)
    turn = (rows[:, None, None] + n_row * jnp.arange(2)[None, None, :] - lane - my_shifts[choice][:, :, None]) % n_col
    turn = (per * choice[:, :, None] + turn // half).reshape(4 * n_row)
    turn = (turn - per * (first[h] + 1)) % child_rows
    tables = [pick, turn, pair, src_row, places // half, has_block[:, r], by_shift[h], by_kind, first[h][None]]
    solved, got = exchange_factor([t.astype(jnp.int32) for t in tables], tiles, lead_front)

    exponent = jnp.floor(jnp.log2(jnp.maximum(jnp.max(jnp.abs(solved), axis=0), 1e-30))) + 1.0
    coded = jnp.clip(jnp.round(solved * jnp.exp2(15.0 - exponent)), -32767.0, 32767.0).astype(jnp.int16)
    tag = exponent.astype(jnp.int16)
    right = jnp.concatenate([coded[:, :T], jnp.broadcast_to(tag[:T], (16, T))], axis=0)
    left = jnp.concatenate([coded[:, T:].T, jnp.broadcast_to(tag[T:, None], (T, T))], axis=1)

    local_rows = jnp.arange(parent_rows)
    row_pick, row_slot, row_valid = [], [], []
    for child in range(2):
        group = by_block[child][local_rows // 2]
        place = (r + n_row * (local_rows % 2) - shifts[child][group]) % n_col
        row_pick.append((r - child * half - place % half) % n_row)
        row_slot.append(2 * ranks[child][group] + local_rows % 2)
        row_valid.append(has_block[child][local_rows // 2])
    row_pick = jnp.stack(row_pick + row_slot + row_valid).astype(jnp.int32)
    col_pick = jnp.concatenate([by_block, has_block.astype(by_block.dtype)]).astype(jnp.int32)
    result = update(
        fill_local.reshape(-1), row_pick, col_pick, left, right, got, own.reshape(-1, T)
    )
    return result.reshape(front.shape)


def solution(mesh):
    placed = (
        P("row", None, None, "col", None, None),
        P("row", None, None, "col", None, None),
        P(),
        P(),
    )
    return jax.shard_map(
        local,
        mesh=mesh,
        in_specs=placed,
        out_specs=P("row", None, None, "col", None, None),
        check_vma=False,
    )
```

```python
import functools
import jax
import jax.numpy as jnp
from jax import lax
from jax.experimental import pallas as pl
from jax.experimental.pallas import tpu as pltpu
from jax.sharding import PartitionSpec as P

T = 128
NB = 12
RHS = 256
WIDE = NB * T + RHS
HI = lax.Precision.HIGHEST
TDOT = (((0,), (0,)), ((), ()))


def split3(x):
    high = x.astype(jnp.bfloat16).astype(jnp.float32)
    rest = x - high
    mid = rest.astype(jnp.bfloat16).astype(jnp.float32)
    return high, mid, rest - mid


def inverse_factor(work, winv):
    sub = lax.broadcasted_iota(jnp.int32, (8, T), 0)
    lane = lax.broadcasted_iota(jnp.int32, (8, T), 1)
    for b in range(T // 8):
        rows = pl.ds(8 * b, 8)
        pa = work[rows, 0:T]
        pw = work[rows, T : 2 * T]
        cols = [jnp.broadcast_to(pa[:, 8 * b + j : 8 * b + j + 1], (8, T)) for j in range(8)]
        scale = jnp.zeros((8, T), jnp.float32)
        for j in range(8):
            pivot = jnp.broadcast_to(cols[j][j : j + 1, :], (8, T))
            root = lax.rsqrt(pivot)
            root = root * (1.5 - 0.5 * pivot * root * root)
            scale = jnp.where(sub == j, root, scale)
            if j == 7:
                break
            factor = jnp.where(sub > j, cols[j] * (root * root), 0.0)
            pa = pa - factor * jnp.broadcast_to(pa[j : j + 1, :], (8, T))
            pw = pw - factor * jnp.broadcast_to(pw[j : j + 1, :], (8, T))
            for m in range(j + 1, 8):
                cols[m] = cols[m] - factor * jnp.broadcast_to(cols[m][j : j + 1, :], (8, T))
        pw = pw * scale
        winv[rows, :] = pw
        if b < T // 8 - 1:
            pa = jnp.where(lane >= 8 * (b + 1), pa * scale, 0.0)
            left = split3(pa)
            right = split3(jnp.concatenate([pa, pw], axis=1))
            lhs = jnp.concatenate([left[0], left[0], left[1], left[1], left[0], left[2]], axis=0)
            rhs = jnp.concatenate([right[0], right[1], right[0], right[1], right[2], right[0]], axis=0)
            change = lax.dot_general(
                lhs.astype(jnp.bfloat16), rhs.astype(jnp.bfloat16), TDOT, preferred_element_type=jnp.float32
            )
            start = 8 * (b + 1)
            work[start:, :] = work[start:, :] - change[start:, :]


MESH = pl.DeviceIdType.MESH
Q = 4
PART = T // Q
GROUPS = 6
REST = 20
LEAD_ROWS = 4
CORNER = NB // 2 + 1
CODED = NB * T
LEFT = CODED + T
RIGHT = CODED + 16
X_START = (-1, 0, 2, 5)
ROW_START = (1, 4, 7, 10)


def exchange_factor_kernel(
    pick, turn, pair, src_row, src_tile, valid, by_shift, by_kind, first, tiles, lead_front, out, got,
    mat, work, winv, acc, packed, lead_slots, z_out, lead_recv, strip, corner_strip, strip_front, corner_front,
    mine, moved, corner, own_sem, lead_send, lead_got, front_send, front_got, strip_sent, strip_got,
    move_send, move_got, ring_send, ring_got, twin_send, twin_got, z_send, z_got, x_send, x_got, row_send, row_got, *buffers,
):
    n_row, n_col = lax.axis_size("row"), lax.axis_size("col")
    z_recv, x_recv, x_out = buffers[:Q], buffers[Q : 2 * Q], buffers[2 * Q :]
    r, c = lax.axis_index("row"), lax.axis_index("col")
    x, z = c // 4, c % 4
    core = r % 2
    step = 1 - 2 * core
    twin = r + step

    def at_col(dx, dz):
        return lax.rem(x + dx + 4, 4) * 4 + lax.rem(z + dz + 4, 4)

    def row_peer(e):
        return lax.rem(r + e, n_row)

    def remote(src, dst, sent, landed, device):
        return pltpu.make_async_remote_copy(
            src_ref=src, dst_ref=dst, send_sem=sent, recv_sem=landed, device_id=device, device_id_type=MESH
        )

    target_row, target_col = c % n_row, 2 * r + c // n_row
    origin_row, origin_col = c // 2, lax.rem(n_row * c + r, n_col)
    moves = (target_row != r) | (target_col != c)

    barrier = pltpu.get_barrier_semaphore()
    for d in range(1, n_col):
        pl.semaphore_signal(barrier, inc=1, device_id={"col": lax.rem(c + d, n_col)}, device_id_type=MESH)
    for e in range(1, n_row):
        pl.semaphore_signal(barrier, inc=1, device_id={"row": row_peer(e)}, device_id_type=MESH)

    @pl.when(moves)
    def _():
        pl.semaphore_signal(
            barrier, inc=1, device_id={"row": origin_row, "col": origin_col}, device_id_type=MESH
        )

    pl.semaphore_wait(barrier, n_col + n_row - 2 + jnp.where(moves, 1, 0))

    def lead_copy(d):
        return remote(
            lead_slots.at[d], lead_recv.at[d], lead_send.at[d], lead_got.at[d], {"col": lax.rem(c + d, n_col)}
        )

    def front_copy(e, whole):
        if whole:
            return remote(
                lead_front.at[0], corner_front.at[r], front_send.at[1, e], front_got.at[1, r], {"row": row_peer(e)}
            )
        return remote(
            lead_front.at[row_peer(e)], strip_front.at[r], front_send.at[0, e], front_got.at[0, r], {"row": row_peer(e)}
        )

    def strip_copy(e, whole):
        if whole:
            return remote(
                lead_slots.at[0], corner_strip.at[r], strip_sent.at[1, e], strip_got.at[1, r], {"row": row_peer(e)}
            )
        return remote(
            lead_slots.at[row_peer(e)], strip.at[r], strip_sent.at[0, e], strip_got.at[0, r], {"row": row_peer(e)}
        )

    for e in range(1, n_row):
        for whole in (False, True):
            front_copy(e, whole).start()

    @pl.loop(0, n_col)
    def _(d):
        for i in range(LEAD_ROWS):
            lead_slots[d, i] = tiles[LEAD_ROWS * first[0] + i, by_shift[d]]

    for d in range(1, n_col):
        lead_copy(d).start()
    lead_recv[0] = lead_slots[0]
    strip_front[r] = lead_front[r]
    corner_front[r] = lead_front[0]

    def z_copy(q, d):
        return remote(
            z_out.at[q, d - 1], z_recv[q].at[d], z_send.at[q, d], z_got.at[q, d], {"col": at_col(0, d)}
        )

    def x_copy(q, d):
        return remote(
            x_out[q % 2].at[d - 1], x_recv[q].at[d], x_send.at[q, d], x_got.at[q, d], {"col": at_col(d, 0)}
        )

    def row_copy(q, e):
        return remote(
            packed.at[e], got.at[q, e], row_send.at[q, e], row_got.at[q, e], {"row": row_peer(e)}
        )

    def row_own(q):
        return pltpu.make_async_copy(packed.at[0], got.at[q, 0], own_sem.at[q])

    def z_start(q):
        for d in range(1, 4):
            z_copy(q, d).start()

    def x_start(q):
        for d in range(1, 4):
            z_copy(q, d).wait_recv()
            if q >= 2:
                x_copy(q - 2, d).wait_send()

        @pl.loop(0, REST)
        def _(i):
            for kind in range(4):
                for d in range(4):
                    tile = z_recv[q][kind, pair[d, kind], i]
                    if d == 0:
                        x_recv[q][d, kind, i] = tile
                    else:
                        x_out[q % 2][d - 1, kind, i] = tile

        for d in range(1, 4):
            x_copy(q, d).start()

    @pl.loop(0, REST)
    def _(i):
        line = lax.rem(LEAD_ROWS * (first[0] + 1) + i, LEAD_ROWS + REST)
        for a in range(2):
            for q in range(Q):
                part = slice(q * PART, (q + 1) * PART)
                z_recv[q][0, a, i] = tiles[line, by_kind[0, a], part]
                for d in range(1, 4):
                    z_out[q, d - 1, a, i] = tiles[line, by_kind[d, a], part]

    z_start(0)
    z_start(1)

    for d in range(1, n_col):
        lead_copy(d).wait()

    @pl.loop(0, n_row)
    def _(b):
        lead_slots[b] = lead_recv[pick[GROUPS + b]]

    for e in range(1, n_row):
        for whole in (False, True):
            strip_copy(e, whole).start()
    strip[r] = lead_slots[r]
    corner_strip[r] = lead_slots[0]
    x_start(0)
    for e in range(1, n_row):
        for whole in (False, True):
            kind, peer = int(whole), row_peer(e)
            remote(
                lead_slots.at[0], corner_strip.at[peer], strip_sent.at[kind, e], strip_got.at[kind, peer], {"row": peer}
            ).wait_recv()
            remote(
                lead_front.at[0], corner_front.at[peer], front_send.at[kind, e], front_got.at[kind, peer], {"row": peer}
            ).wait_recv()

    @pl.loop(0, NB)
    def _(j):
        tile = strip_front[j % 8, j // 8]
        for child in range(2):
            part = strip[src_row[child, j], src_tile[child, j]].astype(jnp.float32)
            tile = tile + jnp.where(valid[child] > 0, part, 0.0)
        mine[pl.ds(pl.multiple_of(j * T, T), T), :] = tile

    def move(k):
        rows = pl.ds(pl.multiple_of(k * T, T), T)
        return remote(
            mine.at[rows], moved.at[rows], move_send.at[k], move_got.at[k], {"row": target_row, "col": target_col}
        )

    @pl.loop(0, CORNER)
    def _(t):
        j = lax.rem(c + t, NB)
        tile = corner_front[j % 8, j // 8]
        for child in range(2):
            tile = tile + corner_strip[src_row[child, j], src_tile[child, j]].astype(jnp.float32)
        corner[c, pl.ds(pl.multiple_of(t * T, T), T), :] = tile

    half_rows = CORNER * T // 2
    part_rows = half_rows // 2
    ring, twins = [], []

    def place(part, along, across):
        return at_col(across, along) if part == 0 else at_col(along, across)

    def piece(block, part, owner):
        return corner.at[block, pl.ds(pl.multiple_of(owner * half_rows + part * part_rows, part_rows), part_rows)]

    def ring_copy(block, part, target):
        ref = piece(block, part, core)
        copy = remote(ref, ref, ring_send.at[len(ring)], ring_got.at[block, part], {"col": target})
        copy.start()
        ring.append(copy)

    def ring_wait(block, part):
        ref = piece(block, part, core)
        remote(ref, ref, ring_send.at[0], ring_got.at[block, part], {"col": at_col(1, 0)}).wait_recv()
        copy = remote(ref, ref, twin_send.at[len(twins)], twin_got.at[block, part], {"row": twin})
        copy.start()
        twins.append(copy)

    for part in range(2):
        ring_copy(c, part, place(part, 1, 0))
        ring_copy(c, part, place(part, -1, 0))
    for part in range(2):
        ring_copy(c, part, place(part, 0, 1))
        ring_copy(c, part, place(part, 0, -1))
    for part in range(2):
        block = place(part, -step, 0)
        ring_wait(block, part)
        ring_copy(block, part, place(part, step, 0))
        ring_copy(block, part, place(part, 0, 1))
        ring_copy(block, part, place(part, 0, -1))
    for part in range(2):
        block = place(part, step, 0)
        ring_wait(block, part)
        ring_copy(block, part, place(part, 0, 1))
        ring_copy(block, part, place(part, 0, -1))
    for part in range(2):
        block = place(part, 2, 0)
        ring_wait(block, part)
        ring_copy(block, part, place(part, 0, 1))
        ring_copy(block, part, place(part, 0, -1))
    for along in (0, -step, step, 2):
        for part in range(2):
            block = place(part, along, -step)
            ring_wait(block, part)
            ring_copy(block, part, place(part, 0, step))
    for along in range(4):
        for across in (step, 2):
            for part in range(2):
                ring_wait(place(part, along, across), part)
    @pl.when(moves)
    def _():
        @pl.loop(0, NB)
        def _(k):
            move(k).start()

    z_start(2)
    z_start(3)
    mat[...] = jnp.zeros_like(mat)
    mat[:, NB * T : NB * T + T] = mine[...]

    @pl.when(jnp.logical_not(moves))
    def _():
        mat[:, NB * T + T :] = mine[...]

    for dx in range(4):
        for dz in range(4):
            if dx or dz:
                for part in range(2):
                    block = at_col(dx, dz)
                    ref = piece(block, part, 1 - core)
                    remote(ref, ref, twin_send.at[0], twin_got.at[block, part], {"row": twin}).wait_recv()

    for d in range(NB):
        for i in range(d, NB):
            if d < 6:
                tile = corner[i - d, d * T : (d + 1) * T, :]
                tile = tile.T if d else tile
            else:
                tile = corner[i, (NB - d) * T : (NB - d + 1) * T, :]
            mat[(i - d) * T : (i - d + 1) * T, i * T : (i + 1) * T] = tile
    row_id = lax.broadcasted_iota(jnp.int32, (T, T), 0)
    col_id = lax.broadcasted_iota(jnp.int32, (T, T), 1)
    chunks = WIDE // 256

    @pl.loop(0, NB)
    def _(k):
        k0 = pl.multiple_of(k * T, T)
        kk = pl.ds(k0, T)

        @pl.when(moves)
        def _():
            move(k).wait_recv()
            mat[kk, NB * T + T :] = moved[kk, :]

        @pl.loop(k // 2, chunks)
        def _(n):
            nn = pl.ds(pl.multiple_of(n * 256, 256), 256)
            acc[...] = mat[kk, nn]

            @pl.loop(0, (k + 3) // 4)
            def _(p):
                pp = pl.ds(pl.multiple_of(p * 512, 512), 512)
                left = mat[pp, kk]
                left = jnp.where(
                    lax.broadcasted_iota(jnp.int32, (512, T), 0) + p * 512 < k0, left, 0.0
                )
                acc[...] -= lax.dot_general(
                    left, mat[pp, nn], TDOT, precision=HI, preferred_element_type=jnp.float32
                )

            mat[kk, nn] = acc[...]

        work[:, 0:T] = mat[kk, kk]
        work[:, T : 2 * T] = jnp.where(row_id == col_id, 1.0, 0.0)
        inverse_factor(work, winv)

        @pl.loop(k // 2, chunks)
        def _(n):
            nn = pl.ds(pl.multiple_of(n * 256, 256), 256)
            mat[kk, nn] = jnp.dot(
                winv[...], mat[kk, nn], precision=HI, preferred_element_type=jnp.float32
            )

        for q in range(Q):

            @pl.when(k == X_START[q])
            def _(q=q):
                x_start(q)

            @pl.when(k == ROW_START[q])
            def _(q=q):
                for d in range(1, 4):
                    x_copy(q, d).wait_recv()
                if q >= 1:
                    row_own(q - 1).wait()
                    for e in range(1, n_row):
                        row_copy(q - 1, e).wait_send()

                @pl.loop(0, n_row * 4)
                def _(i):
                    line = turn[i]
                    for g in range(GROUPS):
                        rest = x_recv[q][pick[16 + g], pick[24 + g], jnp.minimum(line, REST - 1)]
                        first = lead_recv[pick[g], jnp.maximum(line - REST, 0), q * PART : (q + 1) * PART]
                        packed[i // 4, i % 4, g] = jnp.where(line < REST, rest, first)

                row_own(q).start()
                for e in range(1, n_row):
                    row_copy(q, e).start()

    out[...] = mat[:, NB * T :]

    for e in range(1, n_row):
        for whole in (False, True):
            front_copy(e, whole).wait_send()
            strip_copy(e, whole).wait_send()
    for copy in ring + twins:
        copy.wait_send()
    for q in range(Q):
        for d in range(1, 4):
            z_copy(q, d).wait_send()
        if q >= 2:
            for d in range(1, 4):
                x_copy(q, d).wait_send()
        if q == Q - 1:
            row_own(q).wait()
            for e in range(1, n_row):
                row_copy(q, e).wait_send()
        for e in range(1, n_row):
            row_copy(q, e).wait_recv()

    @pl.when(moves)
    def _():
        @pl.loop(0, NB)
        def _(k):
            move(k).wait_send()


def exchange_factor(tables, tiles, lead_front):
    n_row, n_col = lax.axis_size("row"), lax.axis_size("col")
    vmem = pl.BlockSpec(memory_space=pltpu.VMEM)
    smem = pl.BlockSpec(memory_space=pltpu.SMEM)
    hbm = pl.BlockSpec(memory_space=pl.ANY)
    dma = pltpu.SemaphoreType.DMA
    f32, bf16 = jnp.float32, jnp.bfloat16
    return pl.pallas_call(
        exchange_factor_kernel,
        out_shape=(
            jax.ShapeDtypeStruct((NB * T, RHS), f32),
            jax.ShapeDtypeStruct((Q, n_row, 4, GROUPS, PART, T), bf16),
        ),
        in_specs=[smem] * 9 + [vmem, vmem],
        out_specs=(vmem, hbm),
        scratch_shapes=[
            pltpu.VMEM((NB * T, WIDE), f32),
            pltpu.VMEM((T, 2 * T), f32),
            pltpu.VMEM((T, T), f32),
            pltpu.VMEM((T, 256), f32),
            pltpu.VMEM((n_row, 4, GROUPS, PART, T), bf16),
            pltpu.VMEM((n_col, LEAD_ROWS, T, T), bf16),
            pltpu.VMEM((Q, 3, 2, REST, PART, T), bf16),
            pltpu.VMEM((n_col, LEAD_ROWS, T, T), bf16),
            pltpu.VMEM((n_row, LEAD_ROWS, T, T), bf16),
            pltpu.VMEM((n_row, LEAD_ROWS, T, T), bf16),
            pltpu.VMEM((n_row, 2, T, T), f32),
            pltpu.VMEM((n_row, 2, T, T), f32),
            pltpu.VMEM((NB * T, T), f32),
            pltpu.VMEM((NB * T, T), f32),
            pltpu.VMEM((n_col, CORNER * T, T), f32),
            dma((Q,)),
            dma((n_col,)),
            dma((n_col,)),
            dma((2, n_row)),
            dma((2, n_row)),
            dma((2, n_row)),
            dma((2, n_row)),
            dma((NB,)),
            dma((NB,)),
            dma((32,)),
            dma((n_col, 2)),
            dma((32,)),
            dma((n_col, 2)),
            dma((Q, 4)),
            dma((Q, 4)),
            dma((Q, 4)),
            dma((Q, 4)),
            dma((Q, n_row)),
            dma((Q, n_row)),
        ]
        + [pltpu.VMEM((4, 2, REST, PART, T), bf16)] * Q
        + [pltpu.VMEM((4, 4, REST, PART, T), bf16)] * Q
        + [pltpu.VMEM((3, 4, REST, PART, T), bf16)] * 2,
        compiler_params=pltpu.CompilerParams(
            vmem_limit_bytes=62 * 1024 * 1024, collective_id=0, has_side_effects=True
        ),
    )(*tables, tiles, lead_front)


def update_kernel(
    fill, row_pick, col_pick, left, right, got, front, out,
    lbuf, rbuf, rhi, rlo, lhi, llo, acc, lsend, lrecv, rsend, rrecv,
):
    r, c = lax.axis_index("row"), lax.axis_index("col")
    x, z = c // 4, c % 4
    y, core = r // 2, r % 2
    step = 1 - 2 * core

    def at_col(dx, dz):
        return lax.rem(x + dx + 4, 4) * 4 + lax.rem(z + dz + 4, 4)

    def at_row(dy, flip):
        return lax.rem(y + dy, 4) * 2 + (1 - core if flip else core)

    barrier = pltpu.get_barrier_semaphore()
    for d in (1, -1):
        pl.semaphore_signal(barrier, inc=1, device_id={"col": at_col(d, 0)}, device_id_type=MESH)
        pl.semaphore_signal(barrier, inc=1, device_id={"col": at_col(0, d)}, device_id_type=MESH)
    for dy, flip in ((1, False), (2, False), (3, False), (0, True)):
        pl.semaphore_signal(barrier, inc=1, device_id={"row": at_row(dy, flip)}, device_id_type=MESH)
    pl.semaphore_wait(barrier, 8)

    lbuf[c] = left[...]
    rbuf[r] = right[...]
    sent = []

    def send_left(block, part, target):
        copy = pltpu.make_async_remote_copy(
            src_ref=lbuf.at[block, pl.ds(part * 64, 64)],
            dst_ref=lbuf.at[block, pl.ds(part * 64, 64)],
            send_sem=lsend.at[len(sent)],
            recv_sem=lrecv.at[block, part],
            device_id={"col": target},
            device_id_type=MESH,
        )
        copy.start()
        sent.append(copy)

    def wait_left(block, part):
        pltpu.make_async_remote_copy(
            src_ref=lbuf.at[block, pl.ds(part * 64, 64)],
            dst_ref=lbuf.at[block, pl.ds(part * 64, 64)],
            send_sem=lsend.at[0],
            recv_sem=lrecv.at[block, part],
            device_id={"col": at_col(1, 0)},
            device_id_type=MESH,
        ).wait_recv()

    rsent = []

    def send_right(block, target):
        copy = pltpu.make_async_remote_copy(
            src_ref=rbuf.at[block],
            dst_ref=rbuf.at[block],
            send_sem=rsend.at[len(rsent)],
            recv_sem=rrecv.at[block],
            device_id={"row": target},
            device_id_type=MESH,
        )
        copy.start()
        rsent.append(copy)

    def wait_right(block):
        pltpu.make_async_remote_copy(
            src_ref=rbuf.at[block],
            dst_ref=rbuf.at[block],
            send_sem=rsend.at[0],
            recv_sem=rrecv.at[block],
            device_id={"row": at_row(0, True)},
            device_id_type=MESH,
        ).wait_recv()

    def place(part, along, across):
        return at_col(across, along) if part == 0 else at_col(along, across)

    def assemble(first, last):
        @pl.loop(first * 8, last * 8)
        def _(i):
            li, lj = i // 8, i % 8
            for q in range(Q):
                where = pl.ds((li * T + q * PART) * 8 + lj, PART, stride=8)
                value = front[where, :] * fill[i]
                for child in range(2):
                    entry = got[q, row_pick[child, li], row_pick[2 + child, li], col_pick[child, lj]]
                    valid = row_pick[4 + child, li] * col_pick[2 + child, lj]
                    value = value + jnp.where(valid > 0, entry.astype(jnp.float32), 0.0)
                out[where, :] = value

    for part in range(2):
        send_left(c, part, place(part, 1, 0))
        send_left(c, part, place(part, -1, 0))
    send_right(r, at_row(0, True))
    for dy in (1, 3, 2):
        send_right(r, at_row(dy, False))
    for part in range(2):
        send_left(c, part, place(part, 0, 1))
        send_left(c, part, place(part, 0, -1))
    assemble(0, 4)
    for part in range(2):
        block = place(part, -step, 0)
        wait_left(block, part)
        send_left(block, part, place(part, step, 0))
        send_left(block, part, place(part, 0, 1))
        send_left(block, part, place(part, 0, -1))
    for part in range(2):
        block = place(part, step, 0)
        wait_left(block, part)
        send_left(block, part, place(part, 0, 1))
        send_left(block, part, place(part, 0, -1))
    for dy in (1, 3):
        wait_right(at_row(dy, False))
        send_right(at_row(dy, False), at_row(0, True))
    assemble(4, 8)
    for part in range(2):
        block = place(part, 2, 0)
        wait_left(block, part)
        send_left(block, part, place(part, 0, 1))
        send_left(block, part, place(part, 0, -1))
    wait_right(at_row(2, False))
    send_right(at_row(2, False), at_row(0, True))
    assemble(8, 16)
    for dy in range(4):
        wait_right(at_row(dy, True))

    def split(coded, scale):
        value = coded.astype(jnp.int32).astype(jnp.float32) * scale
        high = value.astype(jnp.bfloat16)
        return high, (value - high.astype(jnp.float32)).astype(jnp.bfloat16)

    @pl.loop(0, 8)
    def _(j):
        scale = jnp.exp2(rbuf[j, CODED:RIGHT, :].astype(jnp.int32).astype(jnp.float32)[0:1, :] - 15.0)
        lanes = pl.ds(pl.multiple_of((j % 2) * T, T), T)

        @pl.loop(0, NB)
        def _(k):
            rows = pl.ds(pl.multiple_of(k * T, T), T)
            rhi[j // 2, rows, lanes], rlo[j // 2, rows, lanes] = split(rbuf[j, rows, :], scale)

    def subtract(pieces):
        for m, (li, part) in enumerate(pieces):
            source = pl.ds(part * 64, 64)
            scale = jnp.exp2(lbuf[li, source, CODED:LEFT].astype(jnp.int32).astype(jnp.float32) - 15.0)

            @pl.loop(0, NB)
            def _(k, m=m, li=li, source=source, scale=scale):
                lanes = pl.ds(pl.multiple_of(k * T, T), T)
                high, low = split(lbuf[li, source, lanes], scale)
                lhi[m * 64 : (m + 1) * 64, lanes] = high
                llo[m * 64 : (m + 1) * 64, lanes] = low

        @pl.loop(0, 4)
        def _(n):
            total = jnp.dot(lhi[...], rlo[n], preferred_element_type=jnp.float32)
            total += jnp.dot(llo[...], rhi[n], preferred_element_type=jnp.float32)
            total += jnp.dot(lhi[...], rhi[n], preferred_element_type=jnp.float32)
            acc[...] = total
            for m, (li, part) in enumerate(pieces):
                for j in range(2):
                    lj = n * 2 + j
                    where = pl.ds((li * T + part * 64) * 8 + lj, 64, stride=8)
                    change = acc[m * 64 : (m + 1) * 64, j * T : (j + 1) * T]
                    cleared = (r + 8 * li < NB) & (c + 16 * lj >= NB)
                    out[where, :] = jnp.where(cleared, 0.0, out[where, :] - change)

    def arrived(across):
        return [(place(part, along, across), part) for part in range(2) for along in (0, -step, step, 2)]

    subtract(arrived(0))
    for block, part in arrived(-step):
        wait_left(block, part)
        send_left(block, part, place(part, 0, step))
    subtract(arrived(-step))
    for across in (step, 2):
        for block, part in arrived(across):
            wait_left(block, part)
        subtract(arrived(across))

    row_id = lax.broadcasted_iota(jnp.int32, (T, T), 0)
    col_id = lax.broadcasted_iota(jnp.int32, (T, T), 1)
    panel_lanes = pl.ds(pl.multiple_of(jnp.minimum(c, NB - 1) * T, T), T)

    @pl.when(c < NB)
    def _():
        @pl.loop(0, 16)
        def _(li):
            row_tile = r + 8 * li
            scale = jnp.exp2(lbuf[li, :, CODED:LEFT].astype(jnp.int32).astype(jnp.float32) - 15.0)
            value = lbuf[li, :, panel_lanes].astype(jnp.int32).astype(jnp.float32) * scale
            keep = (row_tile > c) | ((row_tile == c) & (row_id >= col_id))
            out[pl.ds(li * T * 8, T, stride=8), :] = jnp.where(keep, value, 0.0)

    for copy in sent + rsent:
        copy.wait_send()


def update(fill, row_pick, col_pick, left, right, got, front):
    vmem = pl.BlockSpec(memory_space=pltpu.VMEM)
    smem = pl.BlockSpec(memory_space=pltpu.SMEM)
    dma = pltpu.SemaphoreType.DMA
    return pl.pallas_call(
        update_kernel,
        out_shape=jax.ShapeDtypeStruct(front.shape, jnp.float32),
        in_specs=[smem] * 3 + [vmem] * 4,
        out_specs=vmem,
        scratch_shapes=[
            pltpu.VMEM((16, T, LEFT), jnp.int16),
            pltpu.VMEM((8, RIGHT, T), jnp.int16),
            pltpu.VMEM((4, CODED, 256), jnp.bfloat16),
            pltpu.VMEM((4, CODED, 256), jnp.bfloat16),
            pltpu.VMEM((4 * T, CODED), jnp.bfloat16),
            pltpu.VMEM((4 * T, CODED), jnp.bfloat16),
            pltpu.VMEM((4 * T, 256), jnp.float32),
            dma((32,)),
            dma((16, 2)),
            dma((8,)),
            dma((8,)),
        ],
        compiler_params=pltpu.CompilerParams(
            vmem_limit_bytes=60 * 1024 * 1024, collective_id=1, has_side_effects=True
        ),
    )(fill, row_pick, col_pick, left, right, got, front)


def local(front, children, child_maps, fill):
    n_row = lax.axis_size("row")
    n_col = lax.axis_size("col")
    half = n_row // 2
    r = lax.axis_index("row")
    c = lax.axis_index("col")
    h = r // half
    lane = r % half
    tiles = children[0, :, :, 0].transpose(0, 2, 1, 3)
    child_rows, groups = tiles.shape[:2]
    own = front[0, :, :, 0]
    parent_rows, _, parent_cols, _ = own.shape
    per = n_col // half

    heads = child_maps[:, ::n_col]
    shifts = heads % n_col
    blocks = heads // n_col
    wanted = jnp.arange(n_col)
    by_shift = jnp.argmax(shifts[:, None, :] == wanted[None, :, None], axis=2)
    hits = blocks[:, None, :] == jnp.arange(parent_cols)[None, :, None]
    by_block = jnp.argmax(hits, axis=2)
    has_block = jnp.any(hits, axis=2)
    first = by_block[:, 0]

    fill_rows = lax.dynamic_index_in_dim(fill.reshape(parent_rows, n_row, parent_cols, n_col), r, 1, keepdims=False)
    fill_local = lax.dynamic_index_in_dim(fill_rows, c, 2, keepdims=False).astype(jnp.float32)
    base = own[:2] * fill_local[:2, None, :, None]

    lead_front = base.transpose(2, 0, 1, 3)

    ranks = jnp.sum(
        (shifts[:, None, :] % half == shifts[:, :, None] % half)
        & (jnp.arange(groups)[None, None, :] < jnp.arange(groups)[None, :, None]),
        axis=2,
    )
    my_shifts, my_ranks = shifts[h], ranks[h]
    kinds = my_shifts % 4
    chosen = (kinds[None, None, :] == jnp.arange(4)[:, None, None]) & (
        my_ranks[None, None, :] == jnp.arange(2)[None, :, None]
    )
    by_kind = jnp.argmax(chosen, axis=2)
    x, z = c // 4, c % 4
    hops = (my_shifts // 4 + (z < kinds)) % 4
    pair = jnp.sum(
        jnp.where(
            (hops[None, None, :] == jnp.arange(4)[:, None, None])
            & (kinds[None, None, :] == jnp.arange(4)[None, :, None]),
            my_ranks[None, None, :],
            0,
        ),
        axis=2,
    )
    pad = jnp.zeros((2,), jnp.int32)
    pick = jnp.concatenate(
        [my_shifts, my_shifts[by_block[h]], pad, hops, pad, kinds]
    ).astype(jnp.int32)
    places = (wanted[None, :NB] - jnp.take_along_axis(shifts, first[:, None], axis=1)) % n_col
    src_row = half * jnp.arange(2)[:, None] + places % half
    rows = (r + jnp.arange(n_row)) % n_row
    lanes = (lane + my_shifts[None, :]) % half == (rows % half)[:, None]
    choice = jnp.argmax(lanes[:, None, :] & (my_ranks[None, None, :] == jnp.arange(2)[None, :, None]), axis=2)
    turn = (rows[:, None, None] + n_row * jnp.arange(2)[None, None, :] - lane - my_shifts[choice][:, :, None]) % n_col
    turn = (per * choice[:, :, None] + turn // half).reshape(4 * n_row)
    turn = (turn - per * (first[h] + 1)) % child_rows
    tables = [pick, turn, pair, src_row, places // half, has_block[:, r], by_shift[h], by_kind, first[h][None]]
    solved, got = exchange_factor([t.astype(jnp.int32) for t in tables], tiles, lead_front)

    exponent = jnp.floor(jnp.log2(jnp.maximum(jnp.max(jnp.abs(solved), axis=0), 1e-30))) + 1.0
    coded = jnp.clip(jnp.round(solved * jnp.exp2(15.0 - exponent)), -32767.0, 32767.0).astype(jnp.int16)
    tag = exponent.astype(jnp.int16)
    right = jnp.concatenate([coded[:, :T], jnp.broadcast_to(tag[:T], (16, T))], axis=0)
    left = jnp.concatenate([coded[:, T:].T, jnp.broadcast_to(tag[T:, None], (T, T))], axis=1)

    local_rows = jnp.arange(parent_rows)
    row_pick, row_slot, row_valid = [], [], []
    for child in range(2):
        group = by_block[child][local_rows // 2]
        place = (r + n_row * (local_rows % 2) - shifts[child][group]) % n_col
        row_pick.append((r - child * half - place % half) % n_row)
        row_slot.append(2 * ranks[child][group] + local_rows % 2)
        row_valid.append(has_block[child][local_rows // 2])
    row_pick = jnp.stack(row_pick + row_slot + row_valid).astype(jnp.int32)
    col_pick = jnp.concatenate([by_block, has_block.astype(by_block.dtype)]).astype(jnp.int32)
    result = update(
        fill_local.reshape(-1), row_pick, col_pick, left, right, got, own.reshape(-1, T)
    )
    return result.reshape(front.shape)


def solution(mesh):
    placed = (
        P("row", None, None, "col", None, None),
        P("row", None, None, "col", None, None),
        P(),
        P(),
    )
    return jax.shard_map(
        local,
        mesh=mesh,
        in_specs=placed,
        out_specs=P("row", None, None, "col", None, None),
        check_vma=False,
    )
```

```python
import functools
import jax
import jax.numpy as jnp
from jax import lax
from jax.experimental import pallas as pl
from jax.experimental.pallas import tpu as pltpu
from jax.sharding import PartitionSpec as P

T = 128
NB = 12
RHS = 256
WIDE = NB * T + RHS
HI = lax.Precision.HIGHEST
TDOT = (((0,), (0,)), ((), ()))


def split3(x):
    high = x.astype(jnp.bfloat16).astype(jnp.float32)
    rest = x - high
    mid = rest.astype(jnp.bfloat16).astype(jnp.float32)
    return high, mid, rest - mid


def inverse_factor(work, winv):
    sub = lax.broadcasted_iota(jnp.int32, (8, T), 0)
    lane = lax.broadcasted_iota(jnp.int32, (8, T), 1)
    for b in range(T // 8):
        rows = pl.ds(8 * b, 8)
        pa = work[rows, 0:T]
        pw = work[rows, T : 2 * T]
        cols = [jnp.broadcast_to(pa[:, 8 * b + j : 8 * b + j + 1], (8, T)) for j in range(8)]
        scale = jnp.zeros((8, T), jnp.float32)
        for j in range(8):
            pivot = jnp.broadcast_to(cols[j][j : j + 1, :], (8, T))
            root = lax.rsqrt(pivot)
            miss = 1.0 - (pivot * root) * root
            scale = jnp.where(sub == j, root + root * (0.5 * miss), scale)
            if j == 7:
                break
            square = root * root
            factor = jnp.where(sub > j, cols[j], 0.0) * (square + square * miss)
            pa = pa - factor * jnp.broadcast_to(pa[j : j + 1, :], (8, T))
            pw = pw - factor * jnp.broadcast_to(pw[j : j + 1, :], (8, T))
            for m in range(j + 1, 8):
                cols[m] = cols[m] - factor * jnp.broadcast_to(cols[m][j : j + 1, :], (8, T))
        pw = pw * scale
        winv[rows, :] = pw
        if b < T // 8 - 1:
            pa = jnp.where(lane >= 8 * (b + 1), pa * scale, 0.0)
            left = split3(pa)
            right = split3(jnp.concatenate([pa, pw], axis=1))
            lhs = jnp.concatenate([left[0], left[0], left[1], left[1], left[0], left[2]], axis=0)
            rhs = jnp.concatenate([right[0], right[1], right[0], right[1], right[2], right[0]], axis=0)
            change = lax.dot_general(
                lhs.astype(jnp.bfloat16), rhs.astype(jnp.bfloat16), TDOT, preferred_element_type=jnp.float32
            )
            start = 8 * (b + 1)
            work[start:, :] = work[start:, :] - change[start:, :]


MESH = pl.DeviceIdType.MESH
Q = 4
PART = T // Q
GROUPS = 6
REST = 20
LEAD_ROWS = 4
CORNER = NB // 2 + 1
CODED = NB * T
LEFT = CODED + T
RIGHT = CODED + 16
X_START = (-1, 0, 2, 5)
ROW_START = (1, 4, 7, 10)


def exchange_factor_kernel(
    pick, turn, pair, src_row, src_tile, valid, by_shift, by_kind, first, tiles, lead_front, out, got,
    mat, work, winv, acc, packed, lead_slots, z_out, lead_recv, strip, corner_strip, strip_front, corner_front,
    mine, moved, corner, own_sem, lead_send, lead_got, front_send, front_got, strip_sent, strip_got,
    move_send, move_got, ring_send, ring_got, twin_send, twin_got, z_send, z_got, x_send, x_got, row_send, row_got, *buffers,
):
    n_row, n_col = lax.axis_size("row"), lax.axis_size("col")
    z_recv, x_recv, x_out = buffers[:Q], buffers[Q : 2 * Q], buffers[2 * Q :]
    r, c = lax.axis_index("row"), lax.axis_index("col")
    x, z = c // 4, c % 4
    core = r % 2
    step = 1 - 2 * core
    twin = r + step

    def at_col(dx, dz):
        return lax.rem(x + dx + 4, 4) * 4 + lax.rem(z + dz + 4, 4)

    def row_peer(e):
        return lax.rem(r + e, n_row)

    def remote(src, dst, sent, landed, device):
        return pltpu.make_async_remote_copy(
            src_ref=src, dst_ref=dst, send_sem=sent, recv_sem=landed, device_id=device, device_id_type=MESH
        )

    target_row, target_col = c % n_row, 2 * r + c // n_row
    origin_row, origin_col = c // 2, lax.rem(n_row * c + r, n_col)
    moves = (target_row != r) | (target_col != c)

    barrier = pltpu.get_barrier_semaphore()
    for d in range(1, n_col):
        pl.semaphore_signal(barrier, inc=1, device_id={"col": lax.rem(c + d, n_col)}, device_id_type=MESH)
    for e in range(1, n_row):
        pl.semaphore_signal(barrier, inc=1, device_id={"row": row_peer(e)}, device_id_type=MESH)

    @pl.when(moves)
    def _():
        pl.semaphore_signal(
            barrier, inc=1, device_id={"row": origin_row, "col": origin_col}, device_id_type=MESH
        )

    pl.semaphore_wait(barrier, n_col + n_row - 2 + jnp.where(moves, 1, 0))

    def lead_copy(d):
        return remote(
            lead_slots.at[d], lead_recv.at[d], lead_send.at[d], lead_got.at[d], {"col": lax.rem(c + d, n_col)}
        )

    def front_copy(e, whole):
        if whole:
            return remote(
                lead_front.at[0], corner_front.at[r], front_send.at[1, e], front_got.at[1, r], {"row": row_peer(e)}
            )
        return remote(
            lead_front.at[row_peer(e)], strip_front.at[r], front_send.at[0, e], front_got.at[0, r], {"row": row_peer(e)}
        )

    def strip_copy(e, whole):
        if whole:
            return remote(
                lead_slots.at[0], corner_strip.at[r], strip_sent.at[1, e], strip_got.at[1, r], {"row": row_peer(e)}
            )
        return remote(
            lead_slots.at[row_peer(e)], strip.at[r], strip_sent.at[0, e], strip_got.at[0, r], {"row": row_peer(e)}
        )

    for e in range(1, n_row):
        for whole in (False, True):
            front_copy(e, whole).start()

    @pl.loop(0, n_col)
    def _(d):
        for i in range(LEAD_ROWS):
            lead_slots[d, i] = tiles[LEAD_ROWS * first[0] + i, by_shift[d]]

    for d in range(1, n_col):
        lead_copy(d).start()
    lead_recv[0] = lead_slots[0]
    strip_front[r] = lead_front[r]
    corner_front[r] = lead_front[0]

    def z_copy(q, d):
        return remote(
            z_out.at[q, d - 1], z_recv[q].at[d], z_send.at[q, d], z_got.at[q, d], {"col": at_col(0, d)}
        )

    def x_copy(q, d):
        return remote(
            x_out[q % 2].at[d - 1], x_recv[q].at[d], x_send.at[q, d], x_got.at[q, d], {"col": at_col(d, 0)}
        )

    def row_copy(q, e):
        return remote(
            packed.at[e], got.at[q, e], row_send.at[q, e], row_got.at[q, e], {"row": row_peer(e)}
        )

    def row_own(q):
        return pltpu.make_async_copy(packed.at[0], got.at[q, 0], own_sem.at[q])

    def z_start(q):
        for d in range(1, 4):
            z_copy(q, d).start()

    def x_start(q):
        for d in range(1, 4):
            z_copy(q, d).wait_recv()
            if q >= 2:
                x_copy(q - 2, d).wait_send()

        @pl.loop(0, REST)
        def _(i):
            for kind in range(4):
                for d in range(4):
                    tile = z_recv[q][kind, pair[d, kind], i]
                    if d == 0:
                        x_recv[q][d, kind, i] = tile
                    else:
                        x_out[q % 2][d - 1, kind, i] = tile

        for d in range(1, 4):
            x_copy(q, d).start()

    @pl.loop(0, REST)
    def _(i):
        line = lax.rem(LEAD_ROWS * (first[0] + 1) + i, LEAD_ROWS + REST)
        for a in range(2):
            for q in range(Q):
                part = slice(q * PART, (q + 1) * PART)
                z_recv[q][0, a, i] = tiles[line, by_kind[0, a], part]
                for d in range(1, 4):
                    z_out[q, d - 1, a, i] = tiles[line, by_kind[d, a], part]

    z_start(0)
    z_start(1)
    mat[...] = jnp.zeros_like(mat)

    for d in range(1, n_col):
        lead_copy(d).wait()

    @pl.loop(0, n_row)
    def _(b):
        lead_slots[b] = lead_recv[pick[GROUPS + b]]

    for e in range(1, n_row):
        for whole in (False, True):
            strip_copy(e, whole).start()
    strip[r] = lead_slots[r]
    corner_strip[r] = lead_slots[0]
    x_start(0)
    for e in range(1, n_row):
        for whole in (False, True):
            kind, peer = int(whole), row_peer(e)
            remote(
                lead_slots.at[0], corner_strip.at[peer], strip_sent.at[kind, e], strip_got.at[kind, peer], {"row": peer}
            ).wait_recv()
            remote(
                lead_front.at[0], corner_front.at[peer], front_send.at[kind, e], front_got.at[kind, peer], {"row": peer}
            ).wait_recv()

    @pl.loop(0, NB)
    def _(j):
        tile = strip_front[j % 8, j // 8]
        for child in range(2):
            part = strip[src_row[child, j], src_tile[child, j]].astype(jnp.float32)
            tile = tile + jnp.where(valid[child] > 0, part, 0.0)
        mine[pl.ds(pl.multiple_of(j * T, T), T), :] = tile

    def move(k):
        rows = pl.ds(pl.multiple_of(k * T, T), T)
        return remote(
            mine.at[rows], moved.at[rows], move_send.at[k], move_got.at[k], {"row": target_row, "col": target_col}
        )

    @pl.loop(0, CORNER)
    def _(t):
        j = lax.rem(c + t, NB)
        tile = corner_front[j % 8, j // 8]
        for child in range(2):
            tile = tile + corner_strip[src_row[child, j], src_tile[child, j]].astype(jnp.float32)
        corner[c, pl.ds(pl.multiple_of(t * T, T), T), :] = tile

    half_rows = CORNER * T // 2
    part_rows = half_rows // 2
    ring, twins = [], []

    def place(part, along, across):
        return at_col(across, along) if part == 0 else at_col(along, across)

    def piece(block, part, owner):
        return corner.at[block, pl.ds(pl.multiple_of(owner * half_rows + part * part_rows, part_rows), part_rows)]

    def ring_copy(block, part, target):
        ref = piece(block, part, core)
        copy = remote(ref, ref, ring_send.at[len(ring)], ring_got.at[block, part], {"col": target})
        ring.append((copy, block))

        @pl.when(block < NB)
        def _():
            copy.start()

    def ring_wait(block, part):
        ref = piece(block, part, core)
        landed = remote(ref, ref, ring_send.at[0], ring_got.at[block, part], {"col": at_col(1, 0)})
        copy = remote(ref, ref, twin_send.at[len(twins)], twin_got.at[block, part], {"row": twin})
        twins.append((copy, block))

        @pl.when(block < NB)
        def _():
            landed.wait_recv()
            copy.start()

    for part in range(2):
        ring_copy(c, part, place(part, 1, 0))
        ring_copy(c, part, place(part, -1, 0))
    for part in range(2):
        ring_copy(c, part, place(part, 0, 1))
        ring_copy(c, part, place(part, 0, -1))
    for part in range(2):
        block = place(part, -step, 0)
        ring_wait(block, part)
        ring_copy(block, part, place(part, step, 0))
        ring_copy(block, part, place(part, 0, 1))
        ring_copy(block, part, place(part, 0, -1))
    for part in range(2):
        block = place(part, step, 0)
        ring_wait(block, part)
        ring_copy(block, part, place(part, 0, 1))
        ring_copy(block, part, place(part, 0, -1))
    for part in range(2):
        block = place(part, 2, 0)
        ring_wait(block, part)
        ring_copy(block, part, place(part, 0, 1))
        ring_copy(block, part, place(part, 0, -1))
    for along in (0, -step, step, 2):
        for part in range(2):
            block = place(part, along, -step)
            ring_wait(block, part)
            ring_copy(block, part, place(part, 0, step))
    for along in range(4):
        for across in (step, 2):
            for part in range(2):
                ring_wait(place(part, along, across), part)
    @pl.when(moves)
    def _():
        @pl.loop(0, NB)
        def _(k):
            move(k).start()

    z_start(2)
    z_start(3)
    mat[:, NB * T : NB * T + T] = mine[...]

    @pl.when(jnp.logical_not(moves))
    def _():
        mat[:, NB * T + T :] = mine[...]

    for dx in range(4):
        for dz in range(4):
            if dx or dz:
                for part in range(2):
                    block = at_col(dx, dz)
                    ref = piece(block, part, 1 - core)
                    landed = remote(ref, ref, twin_send.at[0], twin_got.at[block, part], {"row": twin})
                    pl.when(block < NB)(landed.wait_recv)

    for d in range(NB):
        for i in range(d, NB):
            if d < 6:
                tile = corner[i - d, d * T : (d + 1) * T, :]
                tile = tile.T if d else tile
            else:
                tile = corner[i, (NB - d) * T : (NB - d + 1) * T, :]
            mat[(i - d) * T : (i - d + 1) * T, i * T : (i + 1) * T] = tile
    row_id = lax.broadcasted_iota(jnp.int32, (T, T), 0)
    col_id = lax.broadcasted_iota(jnp.int32, (T, T), 1)
    chunks = WIDE // 256

    @pl.loop(0, NB)
    def _(k):
        k0 = pl.multiple_of(k * T, T)
        kk = pl.ds(k0, T)

        @pl.when(moves)
        def _():
            move(k).wait_recv()
            mat[kk, NB * T + T :] = moved[kk, :]

        @pl.loop(k // 2, chunks)
        def _(n):
            nn = pl.ds(pl.multiple_of(n * 256, 256), 256)
            acc[...] = mat[kk, nn]

            @pl.loop(0, (k + 3) // 4)
            def _(p):
                pp = pl.ds(pl.multiple_of(p * 512, 512), 512)
                left = mat[pp, kk]
                left = jnp.where(
                    lax.broadcasted_iota(jnp.int32, (512, T), 0) + p * 512 < k0, left, 0.0
                )
                acc[...] -= lax.dot_general(
                    left, mat[pp, nn], TDOT, precision=HI, preferred_element_type=jnp.float32
                )

            mat[kk, nn] = acc[...]

        work[:, 0:T] = mat[kk, kk]
        work[:, T : 2 * T] = jnp.where(row_id == col_id, 1.0, 0.0)
        inverse_factor(work, winv)

        @pl.loop(k // 2, chunks)
        def _(n):
            nn = pl.ds(pl.multiple_of(n * 256, 256), 256)
            mat[kk, nn] = jnp.dot(
                winv[...], mat[kk, nn], precision=HI, preferred_element_type=jnp.float32
            )

        for q in range(Q):

            @pl.when(k == X_START[q])
            def _(q=q):
                x_start(q)

            @pl.when(k == ROW_START[q])
            def _(q=q):
                for d in range(1, 4):
                    x_copy(q, d).wait_recv()
                if q >= 1:
                    row_own(q - 1).wait()
                    for e in range(1, n_row):
                        row_copy(q - 1, e).wait_send()

                @pl.loop(0, n_row * 4)
                def _(i):
                    line = turn[i]
                    for g in range(GROUPS):
                        rest = x_recv[q][pick[16 + g], pick[24 + g], jnp.minimum(line, REST - 1)]
                        first = lead_recv[pick[g], jnp.maximum(line - REST, 0), q * PART : (q + 1) * PART]
                        packed[i // 4, i % 4, g] = jnp.where(line < REST, rest, first)

                row_own(q).start()
                for e in range(1, n_row):
                    row_copy(q, e).start()

    out[...] = mat[:, NB * T :]

    for e in range(1, n_row):
        for whole in (False, True):
            front_copy(e, whole).wait_send()
            strip_copy(e, whole).wait_send()
    for copy, block in ring + twins:
        pl.when(block < NB)(copy.wait_send)
    for q in range(Q):
        for d in range(1, 4):
            z_copy(q, d).wait_send()
        if q >= 2:
            for d in range(1, 4):
                x_copy(q, d).wait_send()
        if q == Q - 1:
            row_own(q).wait()
            for e in range(1, n_row):
                row_copy(q, e).wait_send()
        for e in range(1, n_row):
            row_copy(q, e).wait_recv()

    @pl.when(moves)
    def _():
        @pl.loop(0, NB)
        def _(k):
            move(k).wait_send()


def exchange_factor(tables, tiles, lead_front):
    n_row, n_col = lax.axis_size("row"), lax.axis_size("col")
    vmem = pl.BlockSpec(memory_space=pltpu.VMEM)
    smem = pl.BlockSpec(memory_space=pltpu.SMEM)
    hbm = pl.BlockSpec(memory_space=pl.ANY)
    dma = pltpu.SemaphoreType.DMA
    f32, bf16 = jnp.float32, jnp.bfloat16
    return pl.pallas_call(
        exchange_factor_kernel,
        out_shape=(
            jax.ShapeDtypeStruct((NB * T, RHS), f32),
            jax.ShapeDtypeStruct((Q, n_row, 4, GROUPS, PART, T), bf16),
        ),
        in_specs=[smem] * 9 + [vmem, vmem],
        out_specs=(vmem, hbm),
        scratch_shapes=[
            pltpu.VMEM((NB * T, WIDE), f32),
            pltpu.VMEM((T, 2 * T), f32),
            pltpu.VMEM((T, T), f32),
            pltpu.VMEM((T, 256), f32),
            pltpu.VMEM((n_row, 4, GROUPS, PART, T), bf16),
            pltpu.VMEM((n_col, LEAD_ROWS, T, T), bf16),
            pltpu.VMEM((Q, 3, 2, REST, PART, T), bf16),
            pltpu.VMEM((n_col, LEAD_ROWS, T, T), bf16),
            pltpu.VMEM((n_row, LEAD_ROWS, T, T), bf16),
            pltpu.VMEM((n_row, LEAD_ROWS, T, T), bf16),
            pltpu.VMEM((n_row, 2, T, T), f32),
            pltpu.VMEM((n_row, 2, T, T), f32),
            pltpu.VMEM((NB * T, T), f32),
            pltpu.VMEM((NB * T, T), f32),
            pltpu.VMEM((n_col, CORNER * T, T), f32),
            dma((Q,)),
            dma((n_col,)),
            dma((n_col,)),
            dma((2, n_row)),
            dma((2, n_row)),
            dma((2, n_row)),
            dma((2, n_row)),
            dma((NB,)),
            dma((NB,)),
            dma((32,)),
            dma((n_col, 2)),
            dma((32,)),
            dma((n_col, 2)),
            dma((Q, 4)),
            dma((Q, 4)),
            dma((Q, 4)),
            dma((Q, 4)),
            dma((Q, n_row)),
            dma((Q, n_row)),
        ]
        + [pltpu.VMEM((4, 2, REST, PART, T), bf16)] * Q
        + [pltpu.VMEM((4, 4, REST, PART, T), bf16)] * Q
        + [pltpu.VMEM((3, 4, REST, PART, T), bf16)] * 2,
        compiler_params=pltpu.CompilerParams(
            vmem_limit_bytes=62 * 1024 * 1024, collective_id=0, has_side_effects=True
        ),
    )(*tables, tiles, lead_front)


def update_kernel(
    fill, row_pick, col_pick, left, right, got, front, out,
    lbuf, rbuf, rhi, rlo, lhi, llo, acc, lsend, lrecv, rsend, rrecv,
):
    r, c = lax.axis_index("row"), lax.axis_index("col")
    x, z = c // 4, c % 4
    y, core = r // 2, r % 2
    step = 1 - 2 * core

    def at_col(dx, dz):
        return lax.rem(x + dx + 4, 4) * 4 + lax.rem(z + dz + 4, 4)

    def at_row(dy, flip):
        return lax.rem(y + dy, 4) * 2 + (1 - core if flip else core)

    barrier = pltpu.get_barrier_semaphore()
    for d in (1, -1):
        pl.semaphore_signal(barrier, inc=1, device_id={"col": at_col(d, 0)}, device_id_type=MESH)
        pl.semaphore_signal(barrier, inc=1, device_id={"col": at_col(0, d)}, device_id_type=MESH)
    for dy, flip in ((1, False), (2, False), (3, False), (0, True)):
        pl.semaphore_signal(barrier, inc=1, device_id={"row": at_row(dy, flip)}, device_id_type=MESH)
    pl.semaphore_wait(barrier, 8)

    lbuf[c] = left[...]
    rbuf[r] = right[...]
    sent = []

    def send_left(block, part, target):
        copy = pltpu.make_async_remote_copy(
            src_ref=lbuf.at[block, pl.ds(part * 64, 64)],
            dst_ref=lbuf.at[block, pl.ds(part * 64, 64)],
            send_sem=lsend.at[len(sent)],
            recv_sem=lrecv.at[block, part],
            device_id={"col": target},
            device_id_type=MESH,
        )
        copy.start()
        sent.append(copy)

    def wait_left(block, part):
        pltpu.make_async_remote_copy(
            src_ref=lbuf.at[block, pl.ds(part * 64, 64)],
            dst_ref=lbuf.at[block, pl.ds(part * 64, 64)],
            send_sem=lsend.at[0],
            recv_sem=lrecv.at[block, part],
            device_id={"col": at_col(1, 0)},
            device_id_type=MESH,
        ).wait_recv()

    rsent = []

    def send_right(block, target):
        copy = pltpu.make_async_remote_copy(
            src_ref=rbuf.at[block],
            dst_ref=rbuf.at[block],
            send_sem=rsend.at[len(rsent)],
            recv_sem=rrecv.at[block],
            device_id={"row": target},
            device_id_type=MESH,
        )
        copy.start()
        rsent.append(copy)

    def wait_right(block):
        pltpu.make_async_remote_copy(
            src_ref=rbuf.at[block],
            dst_ref=rbuf.at[block],
            send_sem=rsend.at[0],
            recv_sem=rrecv.at[block],
            device_id={"row": at_row(0, True)},
            device_id_type=MESH,
        ).wait_recv()

    def place(part, along, across):
        return at_col(across, along) if part == 0 else at_col(along, across)

    def assemble(first, last):
        @pl.loop(first * 8, last * 8)
        def _(i):
            li, lj = i // 8, i % 8
            for q in range(Q):
                where = pl.ds((li * T + q * PART) * 8 + lj, PART, stride=8)
                value = front[where, :] * fill[i]
                for child in range(2):
                    entry = got[q, row_pick[child, li], row_pick[2 + child, li], col_pick[child, lj]]
                    valid = row_pick[4 + child, li] * col_pick[2 + child, lj]
                    value = value + jnp.where(valid > 0, entry.astype(jnp.float32), 0.0)
                out[where, :] = value

    for part in range(2):
        send_left(c, part, place(part, 1, 0))
        send_left(c, part, place(part, -1, 0))
    send_right(r, at_row(0, True))
    for dy in (1, 3, 2):
        send_right(r, at_row(dy, False))
    for part in range(2):
        send_left(c, part, place(part, 0, 1))
        send_left(c, part, place(part, 0, -1))
    assemble(0, 4)
    for part in range(2):
        block = place(part, -step, 0)
        wait_left(block, part)
        send_left(block, part, place(part, step, 0))
        send_left(block, part, place(part, 0, 1))
        send_left(block, part, place(part, 0, -1))
    for part in range(2):
        block = place(part, step, 0)
        wait_left(block, part)
        send_left(block, part, place(part, 0, 1))
        send_left(block, part, place(part, 0, -1))
    for dy in (1, 3):
        wait_right(at_row(dy, False))
        send_right(at_row(dy, False), at_row(0, True))
    assemble(4, 8)
    for part in range(2):
        block = place(part, 2, 0)
        wait_left(block, part)
        send_left(block, part, place(part, 0, 1))
        send_left(block, part, place(part, 0, -1))
    wait_right(at_row(2, False))
    send_right(at_row(2, False), at_row(0, True))
    assemble(8, 16)
    for dy in range(4):
        wait_right(at_row(dy, True))

    def split(coded, scale):
        value = coded.astype(jnp.int32).astype(jnp.float32) * scale
        high = value.astype(jnp.bfloat16)
        return high, (value - high.astype(jnp.float32)).astype(jnp.bfloat16)

    @pl.loop(0, 8)
    def _(j):
        scale = jnp.exp2(rbuf[j, CODED:RIGHT, :].astype(jnp.int32).astype(jnp.float32)[0:1, :] - 15.0)
        lanes = pl.ds(pl.multiple_of((j % 2) * T, T), T)

        @pl.loop(0, NB)
        def _(k):
            rows = pl.ds(pl.multiple_of(k * T, T), T)
            rhi[j // 2, rows, lanes], rlo[j // 2, rows, lanes] = split(rbuf[j, rows, :], scale)

    def subtract(pieces):
        for m, (li, part) in enumerate(pieces):
            source = pl.ds(part * 64, 64)
            scale = jnp.exp2(lbuf[li, source, CODED:LEFT].astype(jnp.int32).astype(jnp.float32) - 15.0)

            @pl.loop(0, NB)
            def _(k, m=m, li=li, source=source, scale=scale):
                lanes = pl.ds(pl.multiple_of(k * T, T), T)
                high, low = split(lbuf[li, source, lanes], scale)
                lhi[m * 64 : (m + 1) * 64, lanes] = high
                llo[m * 64 : (m + 1) * 64, lanes] = low

        @pl.loop(0, 4)
        def _(n):
            total = jnp.dot(lhi[...], rlo[n], preferred_element_type=jnp.float32)
            total += jnp.dot(llo[...], rhi[n], preferred_element_type=jnp.float32)
            total += jnp.dot(lhi[...], rhi[n], preferred_element_type=jnp.float32)
            acc[...] = total
            for m, (li, part) in enumerate(pieces):
                for j in range(2):
                    lj = n * 2 + j
                    where = pl.ds((li * T + part * 64) * 8 + lj, 64, stride=8)
                    change = acc[m * 64 : (m + 1) * 64, j * T : (j + 1) * T]
                    cleared = (r + 8 * li < NB) & (c + 16 * lj >= NB)
                    out[where, :] = jnp.where(cleared, 0.0, out[where, :] - change)

    def arrived(across):
        return [(place(part, along, across), part) for part in range(2) for along in (0, -step, step, 2)]

    subtract(arrived(0))
    for block, part in arrived(-step):
        wait_left(block, part)
        send_left(block, part, place(part, 0, step))
    subtract(arrived(-step))
    for across in (step, 2):
        for block, part in arrived(across):
            wait_left(block, part)
        subtract(arrived(across))

    row_id = lax.broadcasted_iota(jnp.int32, (T, T), 0)
    col_id = lax.broadcasted_iota(jnp.int32, (T, T), 1)
    panel_lanes = pl.ds(pl.multiple_of(jnp.minimum(c, NB - 1) * T, T), T)

    @pl.when(c < NB)
    def _():
        @pl.loop(0, 16)
        def _(li):
            row_tile = r + 8 * li
            scale = jnp.exp2(lbuf[li, :, CODED:LEFT].astype(jnp.int32).astype(jnp.float32) - 15.0)
            value = lbuf[li, :, panel_lanes].astype(jnp.int32).astype(jnp.float32) * scale
            keep = (row_tile > c) | ((row_tile == c) & (row_id >= col_id))
            out[pl.ds(li * T * 8, T, stride=8), :] = jnp.where(keep, value, 0.0)

    for copy in sent + rsent:
        copy.wait_send()


def update(fill, row_pick, col_pick, left, right, got, front):
    vmem = pl.BlockSpec(memory_space=pltpu.VMEM)
    smem = pl.BlockSpec(memory_space=pltpu.SMEM)
    dma = pltpu.SemaphoreType.DMA
    return pl.pallas_call(
        update_kernel,
        out_shape=jax.ShapeDtypeStruct(front.shape, jnp.float32),
        in_specs=[smem] * 3 + [vmem] * 4,
        out_specs=vmem,
        scratch_shapes=[
            pltpu.VMEM((16, T, LEFT), jnp.int16),
            pltpu.VMEM((8, RIGHT, T), jnp.int16),
            pltpu.VMEM((4, CODED, 256), jnp.bfloat16),
            pltpu.VMEM((4, CODED, 256), jnp.bfloat16),
            pltpu.VMEM((4 * T, CODED), jnp.bfloat16),
            pltpu.VMEM((4 * T, CODED), jnp.bfloat16),
            pltpu.VMEM((4 * T, 256), jnp.float32),
            dma((32,)),
            dma((16, 2)),
            dma((8,)),
            dma((8,)),
        ],
        compiler_params=pltpu.CompilerParams(
            vmem_limit_bytes=60 * 1024 * 1024, collective_id=1, has_side_effects=True
        ),
    )(fill, row_pick, col_pick, left, right, got, front)


def local(front, children, child_maps, fill):
    n_row = lax.axis_size("row")
    n_col = lax.axis_size("col")
    half = n_row // 2
    r = lax.axis_index("row")
    c = lax.axis_index("col")
    h = r // half
    lane = r % half
    tiles = children[0, :, :, 0].transpose(0, 2, 1, 3)
    child_rows, groups = tiles.shape[:2]
    own = front[0, :, :, 0]
    parent_rows, _, parent_cols, _ = own.shape
    per = n_col // half

    heads = child_maps[:, ::n_col]
    shifts = heads % n_col
    blocks = heads // n_col
    wanted = jnp.arange(n_col)
    by_shift = jnp.argmax(shifts[:, None, :] == wanted[None, :, None], axis=2)
    hits = blocks[:, None, :] == jnp.arange(parent_cols)[None, :, None]
    by_block = jnp.argmax(hits, axis=2)
    has_block = jnp.any(hits, axis=2)
    first = by_block[:, 0]

    fill_rows = lax.dynamic_index_in_dim(fill.reshape(parent_rows, n_row, parent_cols, n_col), r, 1, keepdims=False)
    fill_local = lax.dynamic_index_in_dim(fill_rows, c, 2, keepdims=False).astype(jnp.float32)
    base = own[:2] * fill_local[:2, None, :, None]

    lead_front = base.transpose(2, 0, 1, 3)

    ranks = jnp.sum(
        (shifts[:, None, :] % half == shifts[:, :, None] % half)
        & (jnp.arange(groups)[None, None, :] < jnp.arange(groups)[None, :, None]),
        axis=2,
    )
    my_shifts, my_ranks = shifts[h], ranks[h]
    kinds = my_shifts % 4
    chosen = (kinds[None, None, :] == jnp.arange(4)[:, None, None]) & (
        my_ranks[None, None, :] == jnp.arange(2)[None, :, None]
    )
    by_kind = jnp.argmax(chosen, axis=2)
    x, z = c // 4, c % 4
    hops = (my_shifts // 4 + (z < kinds)) % 4
    pair = jnp.sum(
        jnp.where(
            (hops[None, None, :] == jnp.arange(4)[:, None, None])
            & (kinds[None, None, :] == jnp.arange(4)[None, :, None]),
            my_ranks[None, None, :],
            0,
        ),
        axis=2,
    )
    pad = jnp.zeros((2,), jnp.int32)
    pick = jnp.concatenate(
        [my_shifts, my_shifts[by_block[h]], pad, hops, pad, kinds]
    ).astype(jnp.int32)
    places = (wanted[None, :NB] - jnp.take_along_axis(shifts, first[:, None], axis=1)) % n_col
    src_row = half * jnp.arange(2)[:, None] + places % half
    rows = (r + jnp.arange(n_row)) % n_row
    lanes = (lane + my_shifts[None, :]) % half == (rows % half)[:, None]
    choice = jnp.argmax(lanes[:, None, :] & (my_ranks[None, None, :] == jnp.arange(2)[None, :, None]), axis=2)
    turn = (rows[:, None, None] + n_row * jnp.arange(2)[None, None, :] - lane - my_shifts[choice][:, :, None]) % n_col
    turn = (per * choice[:, :, None] + turn // half).reshape(4 * n_row)
    turn = (turn - per * (first[h] + 1)) % child_rows
    tables = [pick, turn, pair, src_row, places // half, has_block[:, r], by_shift[h], by_kind, first[h][None]]
    solved, got = exchange_factor([t.astype(jnp.int32) for t in tables], tiles, lead_front)

    exponent = jnp.floor(jnp.log2(jnp.maximum(jnp.max(jnp.abs(solved), axis=0), 1e-30))) + 1.0
    coded = jnp.clip(jnp.round(solved * jnp.exp2(15.0 - exponent)), -32767.0, 32767.0).astype(jnp.int16)
    tag = exponent.astype(jnp.int16)
    right = jnp.concatenate([coded[:, :T], jnp.broadcast_to(tag[:T], (16, T))], axis=0)
    left = jnp.concatenate([coded[:, T:].T, jnp.broadcast_to(tag[T:, None], (T, T))], axis=1)

    local_rows = jnp.arange(parent_rows)
    row_pick, row_slot, row_valid = [], [], []
    for child in range(2):
        group = by_block[child][local_rows // 2]
        place = (r + n_row * (local_rows % 2) - shifts[child][group]) % n_col
        row_pick.append((r - child * half - place % half) % n_row)
        row_slot.append(2 * ranks[child][group] + local_rows % 2)
        row_valid.append(has_block[child][local_rows // 2])
    row_pick = jnp.stack(row_pick + row_slot + row_valid).astype(jnp.int32)
    col_pick = jnp.concatenate([by_block, has_block.astype(by_block.dtype)]).astype(jnp.int32)
    result = update(
        fill_local.reshape(-1), row_pick, col_pick, left, right, got, own.reshape(-1, T)
    )
    return result.reshape(front.shape)


def solution(mesh):
    placed = (
        P("row", None, None, "col", None, None),
        P("row", None, None, "col", None, None),
        P(),
        P(),
    )
    return jax.shard_map(
        local,
        mesh=mesh,
        in_specs=placed,
        out_specs=P("row", None, None, "col", None, None),
        check_vma=False,
    )
```
